256 devices in a mesh: ctx: 32 (over z, x), kvh: 8 (over y, core).
Axes of the slice: x: 4, y: 4, z: 8, core: 2. Of those that a mesh axis runs over, the one named last changes fastest.
Arguments:
- queries: float32 [256, 8192], P('ctx', 'kvh'), may hold values from -10 to 10
- cache_keys: float32 [131072, 1024], P('ctx', 'kvh'), may hold values from -12 to 12
- cache_values: float32 [131072, 1024], P('ctx', 'kvh'), may hold values from -6 to 6
- new_keys: float32 [256, 1024], P('ctx', 'kvh'), may hold values from -16 to 16
- new_values: float32 [256, 1024], P('ctx', 'kvh'), may hold values from -6 to 6
- block_lengths: int32 [32], P('ctx'), may hold values from 1 to 4096, 98304 in all
Outputs:
- attended: float32 [256, 8192], P(('ctx', 'kvh'))
The draws below stay inside these ranges and needn't reach their ends.
All inputs are finite; a program needn't handle non-finite values. No bound on the sum of `block_lengths` on one device may be relied on, other than what follows from the above.
Results may differ from the reference program's by a relative error of at most 0.0003.
Values sent between devices are 32-bit elements; how exact they have to be, the bound alone decides.
A program may use at most 128 MiB of HBM per device.

```python
import math
import jax
import jax.numpy as jnp
import numpy as np
from jax import lax

HQ = 64
KVH = 8
HD = 128
BLK = 4096
SPAN = 256
OWNERS = 32
CTX_LEN = 131072


def draw_queries(key, part):
    key = jax.random.fold_in(key, 1)
    base = jnp.clip(jax.random.normal(key, (SPAN, HQ * HD), jnp.float32), -6.0, 6.0)
    return base


def draw_cache_keys(key, part):
    key = jax.random.fold_in(key, 2)
    base = jnp.clip(3.0 * jax.random.normal(key, (CTX_LEN, KVH * HD), jnp.float32), -12.0, 12.0)
    return base


def levels(stream_key, dims, pieces, low, high):
    gain = 1.0
    for dim, blocks in pieces:
        draws = jax.random.uniform(jax.random.fold_in(jax.random.fold_in(stream_key, 6), dim), (blocks,), jnp.float32, low / len(pieces), high / len(pieces))
        gain = gain * jnp.repeat(jnp.exp(draws), dims[dim] // blocks).reshape((-1,) + (1,) * (len(dims) - 1 - dim))
    return gain


def split_up(number_of, total, limit, skew):
    weights = [(1 << 20) // math.isqrt(rank ** skew) + 1 for rank in range(2, number_of + 1)]
    surplus, holding = total - limit - (number_of - 1), [1] * (number_of - 1)
    while surplus > 0:
        free = [i for i in range(number_of - 1) if holding[i] < limit]
        whole, remaining = sum([weights[i] for i in free]), surplus
        for i in free:
            extra = min(limit - holding[i], max(1, remaining * weights[i] // whole), surplus)
            holding[i] = holding[i] + extra
            surplus = surplus - extra
    return np.array([limit] + holding)


def uneven(stream_key, number_of, total, bound, lean):
    if number_of == 2:
        one = jax.random.randint(stream_key, (), max(1, total - bound), min(bound, total - 1) + 1)
        return jnp.stack([one, total - one])
    tallies = jnp.asarray(split_up(number_of, total, bound, lean), jnp.int32)
    pairs = (number_of - 1) // 2
    giver, taker = tallies[1:1 + 2 * pairs:2], tallies[2:2 + 2 * pairs:2]
    margin = jnp.minimum(giver - 1, bound - taker)
    shifted = jax.random.randint(jax.random.fold_in(stream_key, 1), (pairs,), 0, 1 << 20) % (margin + 1)
    tallies = tallies.at[1:1 + 2 * pairs:2].set(giver - shifted).at[2:2 + 2 * pairs:2].set(taker + shifted)
    return tallies[jax.random.permutation(jax.random.fold_in(stream_key, 2), number_of)]


def bell_draw(stream_key, extent, width, bound, cuts=(), held_as=jnp.bfloat16):
    values = jax.random.normal(stream_key, extent, jnp.float32) * width
    if len(cuts) > 0:
        values = levels(stream_key, extent, cuts, -0.22, 0.18) * values
    return jnp.clip(values, min=-bound, max=bound).astype(held_as)


def setup_inputs(seed: int = 0) -> dict:
    arg_keys = jax.random.split(jax.random.key(seed), 7)
    return {
        "queries": draw_queries(jax.random.fold_in(arg_keys[6], 71), 0),
        "cache_keys": draw_cache_keys(jax.random.fold_in(arg_keys[6], 71), 0),
        "cache_values": bell_draw(arg_keys[2], (CTX_LEN, KVH * HD), 1.0, 6.0, ((0, 32), (1, 8)), jnp.float32),
        "new_keys": bell_draw(arg_keys[3], (SPAN, KVH * HD), 4.0, 16.0, ((0, 32), (1, 8)), jnp.float32),
        "new_values": bell_draw(arg_keys[4], (SPAN, KVH * HD), 1.0, 6.0, ((0, 32), (1, 8)), jnp.float32),
        "block_lengths": uneven(arg_keys[5], OWNERS, 3 * OWNERS * BLK // 4, BLK, 2).astype(jnp.int32),
    }


def fold_block(carry, scores, values):
    peak, total, accum = carry
    new_peak = jnp.maximum(peak, jnp.max(scores, axis=-1))
    weights = jnp.exp(scores - new_peak[..., None])
    factor = jnp.exp(peak - new_peak)
    total = total * factor + jnp.sum(weights, axis=-1)
    accum = accum * factor[..., None] + jnp.einsum("gtj,jd->gtd", weights, values, precision=lax.Precision.HIGHEST)
    return new_peak, total, accum


def reference(queries, cache_keys, cache_values, new_keys, new_values, block_lengths):
    group = HQ // KVH
    scale = 1.0 / (HD ** 0.5)
    slots = jnp.arange(BLK).astype(jnp.int32)
    live = slots[None, :] < block_lengths.astype(jnp.int32)[:, None]
    rows = jnp.arange(SPAN).astype(jnp.int32)
    causal = rows[None, :] <= rows[:, None]

    def one_head(index):
        head_q = lax.dynamic_slice_in_dim(queries, index * group * HD, group * HD, 1)
        head_q = head_q.reshape(SPAN, group, HD).transpose(1, 0, 2)
        keys = lax.dynamic_slice_in_dim(cache_keys, index * HD, HD, 1).reshape(OWNERS, BLK, HD)
        values = lax.dynamic_slice_in_dim(cache_values, index * HD, HD, 1).reshape(OWNERS, BLK, HD)
        init = (jnp.full((group, SPAN), -1e30, jnp.float32), jnp.zeros((group, SPAN), jnp.float32), jnp.zeros((group, SPAN, HD), jnp.float32))

        def owner_step(carry, item):
            block_k, block_v, block_live = item
            scores = jnp.einsum("gtd,jd->gtj", head_q, block_k, precision=lax.Precision.HIGHEST) * scale
            scores = jnp.where(block_live[None, None, :], scores, -1e30)
            return fold_block(carry, scores, block_v), None

        carry, unused = lax.scan(owner_step, init, (keys, values, live))
        own_k = lax.dynamic_slice_in_dim(new_keys, index * HD, HD, 1)
        own_v = lax.dynamic_slice_in_dim(new_values, index * HD, HD, 1)
        scores = jnp.einsum("gtd,jd->gtj", head_q, own_k, precision=lax.Precision.HIGHEST) * scale
        scores = jnp.where(causal[None], scores, -1e30)
        peak, total, accum = fold_block(carry, scores, own_v)
        return (accum / total[..., None]).transpose(1, 0, 2)

    heads = lax.map(one_head, jnp.arange(KVH).astype(jnp.int32))
    return heads.transpose(1, 0, 2, 3).reshape(SPAN, HQ * HD)
```

```python
import functools
import math

import jax
import jax.numpy as jnp
from jax import lax
from jax.experimental import pallas as pl
from jax.experimental.pallas import tpu as pltpu
from jax.sharding import PartitionSpec as P

HQ = 64
KVH = 8
HD = 128
GROUP = HQ // KVH
NZ, NX = 8, 4
BLK = 4096
OWN = 8
ROWS = OWN * GROUP
R = NX * ROWS
PIECE = ROWS + 8
NEW = 128
T = 512
SCALE = math.log2(math.e) / math.sqrt(HD)
NEG = -1e30
MESH = pl.DeviceIdType.MESH
bf16, f32 = jnp.bfloat16, jnp.float32
NT = (((1,), (1,)), ((), ()))
NN = (((1,), (0,)), ((), ()))


def dot(a, b, dims):
    return lax.dot_general(a, b, dims, preferred_element_type=f32)


def split(x):
    high = x.astype(bf16)
    return high, (x - high.astype(f32)).astype(bf16)


def halves(k, first):
    return [(k, first), (k, first + 1), (-k, first), (-k, first + 1)]


CHUNKS = [
    [(0, i) for i in range(NX)],
    halves(1, 0),
    halves(2, 0),
    halves(3, 0),
    halves(3, 2),
    [(4, i) for i in range(NX)],
    halves(2, 2),
    halves(1, 2),
]
FORWARD = [(3, 1), (3, 2), (3, 3), (-3, 1), (-3, 2), (-3, 3), (4, 1), (4, 2), (4, 3)]
FAR = [1, -1, 2, -2, 3, -3, 4]
STRAIGHT = halves(1, 2) + halves(2, 2)
ALONG_X = {dz: [1] if abs(dz) < 3 else [1, 2, 3] for dz in FAR}
XSLOT = {pair: i for i, pair in enumerate([(0, k) for k in (1, 2, 3)] + [(dz, dx) for dz in FAR for dx in ALONG_X[dz]])}
DSLOT = {pair: i for i, pair in enumerate(STRAIGHT)}
ZSLOT = {dz: i for i, dz in enumerate(FAR)}


def kernel(
    q_ref, k_ref, v_ref, nk_ref, nv_ref, len_ref, o_ref,
    kbuf, vbuf, kc, vc, qbuf, nkv, sbuf, mbuf, own_o, own_l, own_m, part, xin, din, zout, zin, acc1, acc2,
    otmp, osend, oin,
    ksem, vsem, q_s, q_r, n_s, n_r, x_s, x_r, d_s, d_r, z_s, z_r, o_s, o_r,
):
    c = lax.axis_index("ctx")
    g = lax.axis_index("kvh")
    z, x = c // NX, c % NX

    def ctx_at(dz, dx):
        return {"ctx": ((z + dz + NZ) % NZ) * NX + (x + dx + NX) % NX}

    def remote(src, dst, ssem, rsem, dev):
        return pltpu.make_async_remote_copy(
            src_ref=src, dst_ref=dst, send_sem=ssem, recv_sem=rsem, device_id=dev, device_id_type=MESH
        )

    loads = []
    for i in range(4):
        rows = pl.ds(i * 1024, 1024)
        loads.append(
            (
                pltpu.make_async_copy(k_ref.at[rows], kbuf.at[rows], ksem.at[i]),
                pltpu.make_async_copy(v_ref.at[rows], vbuf.at[rows], vsem.at[i]),
            )
        )
    for one, two in loads:
        one.start()
        two.start()

    offsets = {(0, k) for k in (1, 2, 3)} | {(k, 0) for k in range(1, NZ)}
    for chunk in CHUNKS:
        for dz, dx in chunk:
            if (dz, dx) != (0, 0) and (dz, dx) not in FORWARD:
                offsets |= {(dz % NZ, dx % NX), (-dz % NZ, -dx % NX)}
    for dz, dx in STRAIGHT:
        offsets |= {(dz % NZ, dx % NX), (-dz % NZ, -dx % NX)}
    partners = [ctx_at(*pair) for pair in sorted(offsets, key=lambda pair: (min(pair[0], NZ - pair[0]), pair))]
    partners += [{"kvh": (g + k) % KVH} for k in range(1, KVH)]
    barrier = pltpu.get_barrier_semaphore()
    for dev in partners:
        pl.semaphore_signal(barrier, inc=1, device_id=dev, device_id_type=MESH)

    for h in range(GROUP):
        qbuf[z, x, h * OWN : (h + 1) * OWN, :] = q_ref[:, h * HD : (h + 1) * HD]
    nkv[z, 0:OWN, :] = nk_ref[...]
    nkv[z, OWN : 2 * OWN, :] = nv_ref[...]
    pl.semaphore_wait(barrier, len(partners))

    sent = []

    def go(copy):
        copy.start()
        sent.append(copy)

    def q_copy(dz, dx):
        return remote(
            qbuf.at[z, x], qbuf.at[z, x], q_s.at[dz % NZ, dx], q_r.at[dz % NZ, dx], ctx_at(-dz, -dx)
        )

    def q_pass(dz, dx):
        row = (z + dz + NZ) % NZ
        return remote(
            qbuf.at[row, x], qbuf.at[row, x], q_s.at[dz % NZ, dx], q_r.at[dz % NZ, dx], ctx_at(0, -dx)
        )

    def q_send(pairs):
        for dz, dx in pairs:
            if (dz, dx) != (0, 0) and (dz, dx) not in FORWARD:
                go(q_copy(dz, dx))

    waited = set()

    def q_wait(pairs):
        for pair in pairs:
            if pair != (0, 0) and pair not in waited:
                waited.add(pair)
                q_copy(*pair).wait_recv()

    def q_forward(dz):
        q_wait([(dz, 0)])
        for dx in (1, 2, 3):
            go(q_pass(dz, dx))

    filled = len_ref[0]

    def prep(i, _):
        r = pl.ds(pl.multiple_of(i * 256, 256), 256)
        high, low = split(kbuf[r, :])
        kc[r, 0:128] = high
        kc[r, 128:256] = high
        kc[r, 256:384] = low
        pos = i * 256 + lax.broadcasted_iota(jnp.int32, (256, 128), 0)
        lane = lax.broadcasted_iota(jnp.int32, (256, 128), 1)
        kc[r, 384:512] = jnp.where((lane == 0) & (pos >= filled), NEG, 0.0).astype(bf16)
        high, low = split(vbuf[r, :])
        vc[r, 0:128] = high
        vc[r, 128:256] = low
        return 0

    def prep_part(i):
        loads[i][0].wait()
        loads[i][1].wait()
        lax.fori_loop(i * 4, i * 4 + 4, prep, 0)

    def queries(p):
        rows = [qbuf[(z + dz + NZ) % NZ, (x + dx) % NX] for dz, dx in CHUNKS[p]]
        high, low = split(jnp.concatenate(rows, axis=0) * SCALE)
        lane = lax.broadcasted_iota(jnp.int32, (R, HD), 1)
        return jnp.concatenate([high, low, high, jnp.where(lane == 0, 1.0, 0.0).astype(bf16)], axis=1)

    def fold(s, m, vt, total, acc):
        width = s.shape[1]
        w = jnp.exp2(s - jnp.concatenate([m] * (width // 128), axis=1))
        for i in range(width // 128):
            total = total + w[:, i * 128 : (i + 1) * 128]
        high, low = split(w)
        return total, acc + dot(high, vt, NN) + dot(low, vt, NN)

    def finish(p, out, m, total):
        total = jnp.sum(total, axis=1, keepdims=True)
        lane = lax.broadcasted_iota(jnp.int32, (R, HD), 1)
        both = jnp.where(lane == 0, m, jnp.where(lane == 1, total, 0.0))
        for i in range(NX):
            part[p, i, 0:ROWS, :] = out[i * ROWS : (i + 1) * ROWS]
        for i in range(NX // 2):
            tile = both[i * 128 : (i + 1) * 128].T[0:8]
            part[p, 2 * i, ROWS:PIECE, :] = tile
            part[p, 2 * i + 1, ROWS:PIECE, :] = jnp.concatenate([tile[:, 64:], tile[:, :64]], axis=1)

    def phase(score, attend):
        if score is not None:
            qc = queries(score)
            mx = None
        if attend is not None:
            m = mbuf[attend % 2]
            total = jnp.zeros((R, HD), f32)
            acc = jnp.zeros((R, 2 * HD), f32)
        for j in range(BLK // T):
            t = slice(j * T, (j + 1) * T)
            if attend is not None:
                total, acc = fold(sbuf[:, t], m, vc[t, :], total, acc)
            if score is not None:
                s = dot(qc, kc[t, :], NT)
                sbuf[:, t] = s
                for i in range(T // 128):
                    one = s[:, i * 128 : (i + 1) * 128]
                    mx = one if mx is None else jnp.maximum(mx, one)
        if attend is not None:
            out = acc[:, :HD] + acc[:, HD:]
            if attend == 0:
                own_o[...] = out
                own_l[...] = total
                own_m[...] = m
            else:
                finish(attend, out, m, total)
        if score is not None:
            mbuf[score % 2] = jnp.broadcast_to(jnp.max(mx, axis=1, keepdims=True), (R, HD))

    def new_keys():
        kn = jnp.concatenate(
            [nkv[:, 0:OWN, :].reshape(NZ * OWN, HD), jnp.zeros((NEW - NZ * OWN, HD), f32)], axis=0
        )
        vn = jnp.concatenate(
            [nkv[:, OWN : 2 * OWN, :].reshape(NZ * OWN, HD), jnp.zeros((NEW - NZ * OWN, HD), f32)], axis=0
        )
        high, low = split(kn)
        s = dot(queries(0), jnp.concatenate([high, high, low, jnp.zeros((NEW, HD), bf16)], axis=1), NT)
        row = lax.broadcasted_iota(jnp.int32, (R, NEW), 0)
        col = lax.broadcasted_iota(jnp.int32, (R, NEW), 1)
        token = (z * NX + (x + row // ROWS) % NX) * OWN + row % OWN
        key = ((col // OWN) * NX + x) * OWN + col % OWN
        s = jnp.where((key <= token) & (col < NZ * OWN), s, NEG)
        old = own_m[...]
        m = jnp.maximum(old, jnp.max(s, axis=1, keepdims=True))
        factor = jnp.exp2(old - m)
        high, low = split(vn)
        total, acc = fold(
            s, m, jnp.concatenate([high, low], axis=1), own_l[...] * factor, jnp.zeros((R, 2 * HD), f32)
        )
        finish(0, own_o[...] * factor + acc[:, :HD] + acc[:, HD:], m, total)

    def x_copy(p, i):
        dz, dx = CHUNKS[p][i]
        n = XSLOT[dz, dx]
        return remote(part.at[p, i], xin.at[n], x_s.at[n], x_r.at[n], ctx_at(0, dx))

    def d_copy(p, i):
        dz, dx = CHUNKS[p][i]
        n = DSLOT[dz, dx]
        return remote(part.at[p, i], din.at[n], d_s.at[n], d_r.at[n], ctx_at(dz, dx))

    def z_copy(dz):
        n = ZSLOT[dz]
        return remote(zout.at[n], zin.at[n], z_s.at[n], z_r.at[n], ctx_at(dz, 0))

    arriving = {}

    def send(p):
        for i, pair in enumerate(CHUNKS[p]):
            if pair in XSLOT:
                arriving["x", pair] = x_copy(p, i)
                go(arriving["x", pair])
            if pair in DSLOT:
                arriving["d", pair] = d_copy(p, i)
                go(arriving["d", pair])

    def merge(pieces, last=False):
        tiles = [piece[ROWS:PIECE, :] for piece in pieces]
        peaks = [tile[0:1] for tile in tiles]
        top = functools.reduce(jnp.maximum, peaks)
        factors = [jnp.exp2(one - top) for one in peaks]
        total = functools.reduce(jnp.add, [f * tile[1:2] for f, tile in zip(factors, tiles)])
        if last:
            factors = [f / total for f in factors]
        pad = [jnp.zeros((1, HD), f32)] * (8 - len(factors))
        cols = jnp.concatenate(factors + pad, axis=0).T[0:ROWS]
        out = functools.reduce(
            jnp.add, [cols[:, i : i + 1] * piece[0:ROWS, :] for i, piece in enumerate(pieces)]
        )
        return out, jnp.concatenate([top, total, jnp.zeros((6, HD), f32)], axis=0)

    def merge_to(dst, pieces):
        out, tile = merge(pieces)
        dst[0:ROWS, :] = out
        dst[ROWS:PIECE, :] = tile

    where = {pair: (p, i) for p, chunk in enumerate(CHUNKS) for i, pair in enumerate(chunk)}

    def merge_x(dz):
        pieces = [part.at[where[dz, 0]]]
        for dx in ALONG_X[dz]:
            arriving["x", (dz, dx)].wait_recv()
            pieces.append(xin.at[XSLOT[dz, dx]])
        merge_to(zout.at[ZSLOT[dz]], pieces)
        arriving["z", dz] = z_copy(dz)
        go(arriving["z", dz])

    def z_wait(dz):
        arriving["z", dz].wait_recv()
        return zin.at[ZSLOT[dz]]

    def d_wait(pair):
        arriving["d", pair].wait_recv()
        return din.at[DSLOT[pair]]

    def x_wait(pair):
        arriving["x", pair].wait_recv()
        return xin.at[XSLOT[pair]]

    new_copies = [
        remote(nkv.at[z], nkv.at[z], n_s.at[k - 1], n_r.at[k - 1], ctx_at(k, 0)) for k in range(1, NZ)
    ]

    q_send(CHUNKS[0])
    q_send(CHUNKS[1])
    q_send([(3, 0), (-3, 0)])
    q_send(CHUNKS[2])
    for i in range(4):
        prep_part(i)
    q_send([(4, 0)])
    for copy in new_copies:
        go(copy)
    q_send(CHUNKS[6])
    q_send(CHUNKS[7])

    q_wait(CHUNKS[0])
    phase(0, None)
    phase(None, 0)
    q_wait(CHUNKS[1])
    phase(1, None)
    phase(None, 1)
    send(1)
    q_forward(3)
    q_forward(-3)
    q_wait(CHUNKS[2])
    phase(2, None)
    phase(None, 2)
    send(2)
    for copy in new_copies:
        copy.wait_recv()
    new_keys()
    send(0)
    q_forward(4)
    q_wait(CHUNKS[3])
    phase(3, None)
    merge_x(1)
    merge_x(-1)
    q_wait(CHUNKS[4])
    phase(4, 3)
    send(3)
    merge_x(2)
    merge_x(-2)
    q_wait(CHUNKS[5])
    phase(5, 4)
    send(4)
    q_wait(CHUNKS[6])
    phase(6, 5)
    send(5)
    merge_x(3)
    merge_x(-3)
    phase(None, 6)
    send(6)
    q_wait(CHUNKS[7])
    phase(7, None)
    phase(None, 7)
    send(7)
    merge_x(4)
    pieces = [part.at[0, 0]] + [x_wait((0, dx)) for dx in (1, 2, 3)] + [z_wait(dz) for dz in (1, -1, 2, -2)]
    merge_to(acc1, pieces)
    merge_to(acc2, [acc1] + [z_wait(dz) for dz in (3, -3)] + [d_wait(pair) for pair in halves(2, 2)])
    out, _ = merge([acc2] + [d_wait(pair) for pair in halves(1, 2)] + [z_wait(4)], last=True)

    otmp[...] = out
    for t in range(OWN):
        osend[t] = otmp[pl.ds(t, GROUP, stride=OWN), :]
    o_copies = []
    for k in range(1, KVH):
        there = (g + k) % KVH
        o_copies.append(remote(osend.at[there], oin.at[g], o_s.at[k - 1], o_r.at[k - 1], {"kvh": there}))
    for copy in o_copies:
        go(copy)
    oin[g] = osend[g]
    for copy in o_copies:
        copy.wait_recv()
    o_ref[...] = oin[...].reshape(HQ, HD)
    for copy in sent:
        copy.wait_send()


def per_device(queries, cache_keys, cache_values, new_keys, new_values, block_lengths):
    vmem = pl.BlockSpec(memory_space=pltpu.VMEM)
    hbm = pl.BlockSpec(memory_space=pl.ANY)
    dma = pltpu.SemaphoreType.DMA
    out = pl.pallas_call(
        kernel,
        out_shape=jax.ShapeDtypeStruct((HQ, HD), f32),
        in_specs=[vmem, hbm, hbm, vmem, vmem, pl.BlockSpec(memory_space=pltpu.SMEM)],
        out_specs=vmem,
        scratch_shapes=[
            pltpu.VMEM((BLK, HD), f32),
            pltpu.VMEM((BLK, HD), f32),
            pltpu.VMEM((BLK, 4 * HD), bf16),
            pltpu.VMEM((BLK, 2 * HD), bf16),
            pltpu.VMEM((NZ, NX, ROWS, HD), f32),
            pltpu.VMEM((NZ, 2 * OWN, HD), f32),
            pltpu.VMEM((R, BLK), f32),
            pltpu.VMEM((2, R, HD), f32),
            pltpu.VMEM((R, HD), f32),
            pltpu.VMEM((R, HD), f32),
            pltpu.VMEM((R, HD), f32),
            pltpu.VMEM((len(CHUNKS), NX, PIECE, HD), f32),
            pltpu.VMEM((len(XSLOT), PIECE, HD), f32),
            pltpu.VMEM((len(DSLOT), PIECE, HD), f32),
            pltpu.VMEM((len(ZSLOT), PIECE, HD), f32),
            pltpu.VMEM((len(ZSLOT), PIECE, HD), f32),
            pltpu.VMEM((PIECE, HD), f32),
            pltpu.VMEM((PIECE, HD), f32),
            pltpu.VMEM((ROWS, HD), f32),
            pltpu.VMEM((OWN, GROUP, HD), f32),
            pltpu.VMEM((KVH, GROUP, HD), f32),
            dma((4,)),
            dma((4,)),
            dma((NZ, NX)),
            dma((NZ, NX)),
            dma((NZ - 1,)),
            dma((NZ - 1,)),
            dma((len(XSLOT),)),
            dma((len(XSLOT),)),
            dma((len(DSLOT),)),
            dma((len(DSLOT),)),
            dma((len(ZSLOT),)),
            dma((len(ZSLOT),)),
            dma((KVH - 1,)),
            dma((KVH - 1,)),
        ],
        compiler_params=pltpu.CompilerParams(
            collective_id=0, has_side_effects=True, vmem_limit_bytes=56 * 1024 * 1024
        ),
        cost_estimate=pl.CostEstimate(
            flops=2 * 2 * 2048 * BLK * HD * 3, bytes_accessed=5 * 1024 * 1024, transcendentals=2048 * BLK
        ),
    )(queries, cache_keys, cache_values, new_keys, new_values, block_lengths)
    return out.reshape(1, HQ * HD)


def solution(mesh):
    in_specs = (P("ctx", "kvh"),) * 5 + (P("ctx"),)
    return jax.shard_map(
        per_device, mesh=mesh, in_specs=in_specs, out_specs=P(("ctx", "kvh"), None), check_vma=False
    )
```

```python
import functools
import math

import jax
import jax.numpy as jnp
from jax import lax
from jax.experimental import pallas as pl
from jax.experimental.pallas import tpu as pltpu
from jax.sharding import PartitionSpec as P

HQ = 64
KVH = 8
HD = 128
GROUP = HQ // KVH
NZ, NX = 8, 4
BLK = 4096
OWN = 8
ROWS = OWN * GROUP
R = NX * ROWS
PIECE = ROWS + 8
NEW = 128
T = 512
SCALE = math.log2(math.e) / math.sqrt(HD)
NEG = -1e30
MESH = pl.DeviceIdType.MESH
bf16, f32 = jnp.bfloat16, jnp.float32
NT = (((1,), (1,)), ((), ()))
NN = (((1,), (0,)), ((), ()))


def dot(a, b, dims):
    return lax.dot_general(a, b, dims, preferred_element_type=f32)


def split(x):
    high = x.astype(bf16)
    return high, (x - high.astype(f32)).astype(bf16)


ORDER = [0, 1, -1, 4, 3, -3, 2, -2]
CHUNKS = [[(dz, i) for i in range(NX)] for dz in ORDER]
FAR = ORDER[1:]
XSLOT = {pair: i for i, pair in enumerate([(dz, dx) for dz in ORDER for dx in (1, 2, 3)])}
ZSLOT = {dz: i for i, dz in enumerate(FAR)}


def kernel(
    q_ref, k_ref, v_ref, nk_ref, nv_ref, len_ref, o_ref,
    kbuf, vbuf, kc, vc, qbuf, nkv, sbuf, mbuf, own_o, own_l, own_m, part, xin, zout, zin, acc1, acc2,
    otmp, osend, oin,
    ksem, vsem, q_s, q_r, n_s, n_r, x_s, x_r, z_s, z_r, o_s, o_r,
):
    c = lax.axis_index("ctx")
    g = lax.axis_index("kvh")
    z, x = c // NX, c % NX

    def ctx_at(dz, dx):
        return {"ctx": ((z + dz + NZ) % NZ) * NX + (x + dx + NX) % NX}

    def remote(src, dst, ssem, rsem, dev):
        return pltpu.make_async_remote_copy(
            src_ref=src, dst_ref=dst, send_sem=ssem, recv_sem=rsem, device_id=dev, device_id_type=MESH
        )

    loads = []
    for i in range(4):
        rows = pl.ds(i * 1024, 1024)
        loads.append(
            (
                pltpu.make_async_copy(k_ref.at[rows], kbuf.at[rows], ksem.at[i]),
                pltpu.make_async_copy(v_ref.at[rows], vbuf.at[rows], vsem.at[i]),
            )
        )
    for one, two in loads:
        one.start()
        two.start()

    offsets = {(0, k) for k in (1, 2, 3)} | {(k, 0) for k in range(1, NZ)}
    partners = [ctx_at(*pair) for pair in sorted(offsets, key=lambda pair: (min(pair[0], NZ - pair[0]), pair))]
    partners += [{"kvh": (g + k) % KVH} for k in range(1, KVH)]
    barrier = pltpu.get_barrier_semaphore()
    for dev in partners:
        pl.semaphore_signal(barrier, inc=1, device_id=dev, device_id_type=MESH)

    for h in range(GROUP):
        qbuf[z, x, h * OWN : (h + 1) * OWN, :] = q_ref[:, h * HD : (h + 1) * HD]
    nkv[z, 0:OWN, :] = nk_ref[...]
    nkv[z, OWN : 2 * OWN, :] = nv_ref[...]

    sent = []

    def go(copy):
        copy.start()
        sent.append(copy)

    def own_copy(dx):
        return remote(qbuf.at[z, x], qbuf.at[z, x], q_s.at[0, dx], q_r.at[0, dx], ctx_at(0, -dx))

    def row_copy(dz):
        side = 1 if dz > 0 else -1
        row = qbuf.at[(z + dz - side + NZ) % NZ]
        return remote(row, row, q_s.at[dz % NZ, 0], q_r.at[dz % NZ, 0], ctx_at(-side, 0))

    def far_copy(dz):
        return remote(qbuf.at[z, x], qbuf.at[z, x], q_s.at[dz % NZ, 0], q_r.at[dz % NZ, 0], ctx_at(-dz, 0))

    def pass_copy(dz, dx):
        block = qbuf.at[(z + dz + NZ) % NZ, x]
        return remote(block, block, q_s.at[dz % NZ, dx], q_r.at[dz % NZ, dx], ctx_at(0, -dx))

    filled = len_ref[0]

    def prep(i, _):
        r = pl.ds(pl.multiple_of(i * 256, 256), 256)
        high, low = split(kbuf[r, :])
        kc[r, 0:128] = high
        kc[r, 128:256] = high
        kc[r, 256:384] = low
        pos = i * 256 + lax.broadcasted_iota(jnp.int32, (256, 128), 0)
        lane = lax.broadcasted_iota(jnp.int32, (256, 128), 1)
        kc[r, 384:512] = jnp.where((lane == 0) & (pos >= filled), NEG, 0.0).astype(bf16)
        high, low = split(vbuf[r, :])
        vc[r, 0:128] = high
        vc[r, 128:256] = low
        return 0

    def prep_part(i):
        loads[i][0].wait()
        loads[i][1].wait()
        lax.fori_loop(i * 4, i * 4 + 4, prep, 0)

    def queries(p):
        rows = [qbuf[(z + dz + NZ) % NZ, (x + dx) % NX] for dz, dx in CHUNKS[p]]
        high, low = split(jnp.concatenate(rows, axis=0) * SCALE)
        lane = lax.broadcasted_iota(jnp.int32, (R, HD), 1)
        return jnp.concatenate([high, low, high, jnp.where(lane == 0, 1.0, 0.0).astype(bf16)], axis=1)

    def fold(s, m, vt, total, acc):
        width = s.shape[1]
        w = jnp.exp2(s - jnp.concatenate([m] * (width // 128), axis=1))
        for i in range(width // 128):
            total = total + w[:, i * 128 : (i + 1) * 128]
        high, low = split(w)
        return total, acc + dot(high, vt, NN) + dot(low, vt, NN)

    def finish(p, out, m, total):
        total = jnp.sum(total, axis=1, keepdims=True)
        lane = lax.broadcasted_iota(jnp.int32, (R, HD), 1)
        both = jnp.where(lane == 0, m, jnp.where(lane == 1, total, 0.0))
        for i in range(NX):
            part[p, i, 0:ROWS, :] = out[i * ROWS : (i + 1) * ROWS]
        for i in range(NX // 2):
            tile = both[i * 128 : (i + 1) * 128].T[0:8]
            part[p, 2 * i, ROWS:PIECE, :] = tile
            part[p, 2 * i + 1, ROWS:PIECE, :] = jnp.concatenate([tile[:, 64:], tile[:, :64]], axis=1)

    def phase(score, attend):
        if score is not None:
            qc = queries(score)
            mx = None
        if attend is not None:
            m = mbuf[attend % 2]
            total = jnp.zeros((R, HD), f32)
            acc = jnp.zeros((R, 2 * HD), f32)
        for j in range(BLK // T):
            t = slice(j * T, (j + 1) * T)
            if attend is not None:
                total, acc = fold(sbuf[:, t], m, vc[t, :], total, acc)
            if score is not None:
                s = dot(qc, kc[t, :], NT)
                sbuf[:, t] = s
                for i in range(T // 128):
                    one = s[:, i * 128 : (i + 1) * 128]
                    mx = one if mx is None else jnp.maximum(mx, one)
        if attend is not None:
            out = acc[:, :HD] + acc[:, HD:]
            if attend == 0:
                own_o[...] = out
                own_l[...] = total
                own_m[...] = m
            else:
                finish(attend, out, m, total)
        if score is not None:
            mbuf[score % 2] = jnp.broadcast_to(jnp.max(mx, axis=1, keepdims=True), (R, HD))

    def new_keys():
        kn = jnp.concatenate(
            [nkv[:, 0:OWN, :].reshape(NZ * OWN, HD), jnp.zeros((NEW - NZ * OWN, HD), f32)], axis=0
        )
        vn = jnp.concatenate(
            [nkv[:, OWN : 2 * OWN, :].reshape(NZ * OWN, HD), jnp.zeros((NEW - NZ * OWN, HD), f32)], axis=0
        )
        high, low = split(kn)
        s = dot(queries(0), jnp.concatenate([high, high, low, jnp.zeros((NEW, HD), bf16)], axis=1), NT)
        row = lax.broadcasted_iota(jnp.int32, (R, NEW), 0)
        col = lax.broadcasted_iota(jnp.int32, (R, NEW), 1)
        token = (z * NX + (x + row // ROWS) % NX) * OWN + row % OWN
        key = ((col // OWN) * NX + x) * OWN + col % OWN
        s = jnp.where((key <= token) & (col < NZ * OWN), s, NEG)
        old = own_m[...]
        m = jnp.maximum(old, jnp.max(s, axis=1, keepdims=True))
        factor = jnp.exp2(old - m)
        high, low = split(vn)
        total, acc = fold(
            s, m, jnp.concatenate([high, low], axis=1), own_l[...] * factor, jnp.zeros((R, 2 * HD), f32)
        )
        finish(0, own_o[...] * factor + acc[:, :HD] + acc[:, HD:], m, total)

    def x_copy(p, i):
        dz, dx = CHUNKS[p][i]
        n = XSLOT[dz, dx]
        return remote(part.at[p, i], xin.at[n], x_s.at[n], x_r.at[n], ctx_at(0, dx))

    def z_copy(dz):
        n = ZSLOT[dz]
        return remote(zout.at[n], zin.at[n], z_s.at[n], z_r.at[n], ctx_at(dz, 0))

    arriving = {}

    def send(p):
        for i, pair in enumerate(CHUNKS[p]):
            if pair in XSLOT:
                arriving["x", pair] = x_copy(p, i)
                go(arriving["x", pair])

    def merge(pieces, last=False):
        tiles = [piece[ROWS:PIECE, :] for piece in pieces]
        peaks = [tile[0:1] for tile in tiles]
        top = functools.reduce(jnp.maximum, peaks)
        factors = [jnp.exp2(one - top) for one in peaks]
        total = functools.reduce(jnp.add, [f * tile[1:2] for f, tile in zip(factors, tiles)])
        if last:
            factors = [f / total for f in factors]
        pad = [jnp.zeros((1, HD), f32)] * (8 - len(factors))
        cols = jnp.concatenate(factors + pad, axis=0).T[0:ROWS]
        out = functools.reduce(
            jnp.add, [cols[:, i : i + 1] * piece[0:ROWS, :] for i, piece in enumerate(pieces)]
        )
        return out, jnp.concatenate([top, total, jnp.zeros((6, HD), f32)], axis=0)

    def merge_to(dst, pieces):
        out, tile = merge(pieces)
        dst[0:ROWS, :] = out
        dst[ROWS:PIECE, :] = tile

    where = {pair: (p, i) for p, chunk in enumerate(CHUNKS) for i, pair in enumerate(chunk)}

    def merge_x(dz):
        pieces = [part.at[where[dz, 0]]]
        for dx in (1, 2, 3):
            arriving["x", (dz, dx)].wait_recv()
            pieces.append(xin.at[XSLOT[dz, dx]])
        merge_to(zout.at[ZSLOT[dz]], pieces)

    def send_z(*dzs):
        for dz in dzs:
            arriving["z", dz] = z_copy(dz)
            go(arriving["z", dz])

    def z_wait(dz):
        arriving["z", dz].wait_recv()
        return zin.at[ZSLOT[dz]]

    def x_wait(pair):
        arriving["x", pair].wait_recv()
        return xin.at[XSLOT[pair]]

    new_copies = [
        remote(nkv.at[z], nkv.at[z], n_s.at[k - 1], n_r.at[k - 1], ctx_at(k, 0)) for k in range(1, NZ)
    ]

    for i in range(4):
        prep_part(i)
    pl.semaphore_wait(barrier, len(partners))
    own = [own_copy(dx) for dx in (1, 2, 3)]
    for copy in own:
        go(copy)
    far = {dz: far_copy(dz) for dz in (4, 3, -3)}
    for copy in far.values():
        go(copy)
    for copy in own:
        copy.wait_recv()
    rows = {dz: row_copy(dz) for dz in (1, -1, 2, -2)}
    go(rows[1])
    go(rows[-1])
    phase(0, None)
    phase(None, 0)
    passed = {(dz, dx): pass_copy(dz, dx) for dz in far for dx in (1, 2, 3)}
    for dz in far:
        far[dz].wait_recv()
        for dx in (1, 2, 3):
            go(passed[dz, dx])
    rows[1].wait_recv()
    go(rows[2])
    phase(1, None)
    rows[-1].wait_recv()
    go(rows[-2])
    for copy in new_copies:
        go(copy)
    phase(2, 1)
    send(1)

    def wait_passed(dz):
        for dx in (1, 2, 3):
            passed[dz, dx].wait_recv()

    wait_passed(4)
    phase(3, 2)
    send(2)
    wait_passed(3)
    phase(4, 3)
    send(3)
    for copy in new_copies:
        copy.wait_recv()
    new_keys()
    send(0)
    wait_passed(-3)
    merge_x(1)
    phase(5, 4)
    send(4)
    send_z(1)
    rows[2].wait_recv()
    merge_x(-1)
    merge_x(4)
    phase(6, 5)
    send(5)
    send_z(-1, 4)
    rows[-2].wait_recv()
    merge_x(3)
    phase(7, 6)
    send(6)
    send_z(3)
    phase(None, 7)
    send(7)
    merge_x(-3)
    send_z(-3)
    pieces = [part.at[0, 0]] + [x_wait((0, dx)) for dx in (1, 2, 3)] + [z_wait(dz) for dz in (1, -1, 4)]
    merge_to(acc1, pieces)
    merge_x(2)
    send_z(2)
    merge_to(acc2, [acc1] + [z_wait(dz) for dz in (3, -3)])
    merge_x(-2)
    send_z(-2)
    out, _ = merge([acc2, z_wait(2), z_wait(-2)], last=True)

    otmp[...] = out
    for t in range(OWN):
        osend[t] = otmp[pl.ds(t, GROUP, stride=OWN), :]
    o_copies = []
    for k in range(1, KVH):
        there = (g + k) % KVH
        o_copies.append(remote(osend.at[there], oin.at[g], o_s.at[k - 1], o_r.at[k - 1], {"kvh": there}))
    for copy in o_copies:
        go(copy)
    oin[g] = osend[g]
    for copy in o_copies:
        copy.wait_recv()
    o_ref[...] = oin[...].reshape(HQ, HD)
    for copy in sent:
        copy.wait_send()


def per_device(queries, cache_keys, cache_values, new_keys, new_values, block_lengths):
    vmem = pl.BlockSpec(memory_space=pltpu.VMEM)
    hbm = pl.BlockSpec(memory_space=pl.ANY)
    dma = pltpu.SemaphoreType.DMA
    out = pl.pallas_call(
        kernel,
        out_shape=jax.ShapeDtypeStruct((HQ, HD), f32),
        in_specs=[vmem, hbm, hbm, vmem, vmem, pl.BlockSpec(memory_space=pltpu.SMEM)],
        out_specs=vmem,
        scratch_shapes=[
            pltpu.VMEM((BLK, HD), f32),
            pltpu.VMEM((BLK, HD), f32),
            pltpu.VMEM((BLK, 4 * HD), bf16),
            pltpu.VMEM((BLK, 2 * HD), bf16),
            pltpu.VMEM((NZ, NX, ROWS, HD), f32),
            pltpu.VMEM((NZ, 2 * OWN, HD), f32),
            pltpu.VMEM((R, BLK), f32),
            pltpu.VMEM((2, R, HD), f32),
            pltpu.VMEM((R, HD), f32),
            pltpu.VMEM((R, HD), f32),
            pltpu.VMEM((R, HD), f32),
            pltpu.VMEM((len(CHUNKS), NX, PIECE, HD), f32),
            pltpu.VMEM((len(XSLOT), PIECE, HD), f32),
            pltpu.VMEM((len(ZSLOT), PIECE, HD), f32),
            pltpu.VMEM((len(ZSLOT), PIECE, HD), f32),
            pltpu.VMEM((PIECE, HD), f32),
            pltpu.VMEM((PIECE, HD), f32),
            pltpu.VMEM((ROWS, HD), f32),
            pltpu.VMEM((OWN, GROUP, HD), f32),
            pltpu.VMEM((KVH, GROUP, HD), f32),
            dma((4,)),
            dma((4,)),
            dma((NZ, NX)),
            dma((NZ, NX)),
            dma((NZ - 1,)),
            dma((NZ - 1,)),
            dma((len(XSLOT),)),
            dma((len(XSLOT),)),
            dma((len(ZSLOT),)),
            dma((len(ZSLOT),)),
            dma((KVH - 1,)),
            dma((KVH - 1,)),
        ],
        compiler_params=pltpu.CompilerParams(
            collective_id=0, has_side_effects=True, vmem_limit_bytes=56 * 1024 * 1024
        ),
        cost_estimate=pl.CostEstimate(
            flops=2 * 2 * 2048 * BLK * HD * 3, bytes_accessed=5 * 1024 * 1024, transcendentals=2048 * BLK
        ),
    )(queries, cache_keys, cache_values, new_keys, new_values, block_lengths)
    return out.reshape(1, HQ * HD)


def solution(mesh):
    in_specs = (P("ctx", "kvh"),) * 5 + (P("ctx"),)
    return jax.shard_map(
        per_device, mesh=mesh, in_specs=in_specs, out_specs=P(("ctx", "kvh"), None), check_vma=False
    )
```

```python
import functools
import math

import jax
import jax.numpy as jnp
from jax import lax
from jax.experimental import pallas as pl
from jax.experimental.pallas import tpu as pltpu
from jax.sharding import PartitionSpec as P

HQ = 64
KVH = 8
HD = 128
GROUP = HQ // KVH
NZ, NX = 8, 4
BLK = 4096
OWN = 8
ROWS = OWN * GROUP
R = NX * ROWS
PIECE = ROWS + 8
NEW = 128
T = 512
SCALE = math.log2(math.e) / math.sqrt(HD)
NEG = -1e30
MESH = pl.DeviceIdType.MESH
bf16, f32 = jnp.bfloat16, jnp.float32
NT = (((1,), (1,)), ((), ()))
NN = (((1,), (0,)), ((), ()))


def dot(a, b, dims):
    return lax.dot_general(a, b, dims, preferred_element_type=f32)


def split(x):
    high = x.astype(bf16)
    return high, (x - high.astype(f32)).astype(bf16)


ORDER = [0, 1, -1, 4, 3, -3, 2, -2]
CHUNKS = [[(dz, i) for i in range(NX)] for dz in ORDER]
FAR = ORDER[1:]
XSLOT = {pair: i for i, pair in enumerate([(dz, dx) for dz in ORDER for dx in (1, 2, 3)])}
ZSLOT = {dz: i for i, dz in enumerate(FAR)}


def kernel(
    q_ref, k_ref, v_ref, nk_ref, nv_ref, len_ref, o_ref,
    qin, kbuf, vbuf, kc, vc, qbuf, nkv, sbuf, mbuf, own_o, own_l, own_m, part, xin, zout, zin, acc1,
    otmp, omax, osend, oin,
    in_s, ksem, vsem, q_s, q_r, n_s, n_r, x_s, x_r, z_s, z_r, o_s, o_r,
):
    c = lax.axis_index("ctx")
    g = lax.axis_index("kvh")
    z, x = c // NX, c % NX

    def ctx_at(dz, dx):
        return {"ctx": ((z + dz + NZ) % NZ) * NX + (x + dx + NX) % NX}

    def remote(src, dst, ssem, rsem, dev):
        return pltpu.make_async_remote_copy(
            src_ref=src, dst_ref=dst, send_sem=ssem, recv_sem=rsem, device_id=dev, device_id_type=MESH
        )

    offsets = {(0, k) for k in (1, 2, 3)} | {(k, 0) for k in range(1, NZ)}
    partners = [ctx_at(*pair) for pair in sorted(offsets, key=lambda pair: (min(pair[0], NZ - pair[0]), pair))]
    partners += [{"kvh": (g + k) % KVH} for k in range(1, KVH)]
    partners += [{**ctx_at(dz, 0), "kvh": (g + k) % KVH} for dz in (2, -2) for k in range(1, KVH)]
    barrier = pltpu.get_barrier_semaphore()
    for dev in partners:
        pl.semaphore_signal(barrier, inc=1, device_id=dev, device_id_type=MESH)

    firsts = [
        pltpu.make_async_copy(q_ref, qin, in_s.at[0]),
        pltpu.make_async_copy(nk_ref, nkv.at[z, 0:OWN], in_s.at[1]),
        pltpu.make_async_copy(nv_ref, nkv.at[z, OWN : 2 * OWN], in_s.at[2]),
    ]
    for copy in firsts:
        copy.start()
    loads = []
    for i in range(4):
        rows = pl.ds(i * 1024, 1024)
        loads.append(
            (
                pltpu.make_async_copy(k_ref.at[rows], kbuf.at[rows], ksem.at[i]),
                pltpu.make_async_copy(v_ref.at[rows], vbuf.at[rows], vsem.at[i]),
            )
        )
    for one, two in loads:
        one.start()
        two.start()

    for copy in firsts:
        copy.wait()
    for h in range(GROUP):
        qbuf[z, x, h * OWN : (h + 1) * OWN, :] = qin[:, h * HD : (h + 1) * HD]

    sent = []

    def go(copy):
        copy.start()
        sent.append(copy)

    def own_copy(dx):
        return remote(qbuf.at[z, x], qbuf.at[z, x], q_s.at[0, dx], q_r.at[0, dx], ctx_at(0, -dx))

    def near_copy(dz, dx):
        block = qbuf.at[z, (x + dx) % NX]
        return remote(block, block, q_s.at[dz % NZ, dx], q_r.at[dz % NZ, dx], ctx_at(-dz, 0))

    def row_copy(dz):
        side = 1 if dz > 0 else -1
        row = qbuf.at[(z + dz - side + NZ) % NZ]
        return remote(row, row, q_s.at[dz % NZ, 0], q_r.at[dz % NZ, 0], ctx_at(-side, 0))

    def far_copy(dz):
        return remote(qbuf.at[z, x], qbuf.at[z, x], q_s.at[dz % NZ, 0], q_r.at[dz % NZ, 0], ctx_at(-dz, 0))

    def pass_copy(dz, dx):
        block = qbuf.at[(z + dz + NZ) % NZ, x]
        return remote(block, block, q_s.at[dz % NZ, dx], q_r.at[dz % NZ, dx], ctx_at(0, -dx))

    filled = len_ref[0]

    def prep(i, _):
        r = pl.ds(pl.multiple_of(i * 256, 256), 256)
        high, low = split(kbuf[r, :])
        kc[r, 0:128] = high
        kc[r, 128:256] = high
        kc[r, 256:384] = low
        pos = i * 256 + lax.broadcasted_iota(jnp.int32, (256, 128), 0)
        lane = lax.broadcasted_iota(jnp.int32, (256, 128), 1)
        kc[r, 384:512] = jnp.where((lane == 0) & (pos >= filled), NEG, 0.0).astype(bf16)
        high, low = split(vbuf[r, :])
        vc[r, 0:128] = high
        vc[r, 128:256] = low
        return 0

    def prep_part(i):
        loads[i][0].wait()
        loads[i][1].wait()
        lax.fori_loop(i * 4, i * 4 + 4, prep, 0)

    def queries(p):
        rows = [qbuf[(z + dz + NZ) % NZ, (x + dx) % NX] for dz, dx in CHUNKS[p]]
        high, low = split(jnp.concatenate(rows, axis=0) * SCALE)
        lane = lax.broadcasted_iota(jnp.int32, (R, HD), 1)
        return jnp.concatenate([high, low, high, jnp.where(lane == 0, 1.0, 0.0).astype(bf16)], axis=1)

    def fold(s, m, vt, total, acc):
        width = s.shape[1]
        w = jnp.exp2(s - jnp.concatenate([m] * (width // 128), axis=1))
        for i in range(width // 128):
            total = total + w[:, i * 128 : (i + 1) * 128]
        high, low = split(w)
        return total, acc + dot(high, vt, NN) + dot(low, vt, NN)

    def finish(p, out, m, total):
        total = jnp.sum(total, axis=1, keepdims=True)
        lane = lax.broadcasted_iota(jnp.int32, (R, HD), 1)
        both = jnp.where(lane == 0, m, jnp.where(lane == 1, total, 0.0))
        for i in range(NX):
            part[p, i, 0:ROWS, :] = out[i * ROWS : (i + 1) * ROWS]
        for i in range(NX // 2):
            tile = both[i * 128 : (i + 1) * 128].T[0:8]
            part[p, 2 * i, ROWS:PIECE, :] = tile
            part[p, 2 * i + 1, ROWS:PIECE, :] = jnp.concatenate([tile[:, 64:], tile[:, :64]], axis=1)

    def phase(score, attend):
        if score is not None:
            qc = queries(score)
            mx = None
        if attend is not None:
            m = mbuf[attend % 2]
            total = jnp.zeros((R, HD), f32)
            acc = jnp.zeros((R, 2 * HD), f32)
        for j in range(BLK // T):
            t = slice(j * T, (j + 1) * T)
            if attend is not None:
                total, acc = fold(sbuf[:, t], m, vc[t, :], total, acc)
            if score is not None:
                s = dot(qc, kc[t, :], NT)
                sbuf[:, t] = s
                for i in range(T // 128):
                    one = s[:, i * 128 : (i + 1) * 128]
                    mx = one if mx is None else jnp.maximum(mx, one)
        if attend is not None:
            out = acc[:, :HD] + acc[:, HD:]
            if attend == 0:
                own_o[...] = out
                own_l[...] = total
                own_m[...] = m
            else:
                finish(attend, out, m, total)
        if score is not None:
            mbuf[score % 2] = jnp.broadcast_to(jnp.max(mx, axis=1, keepdims=True), (R, HD))

    def new_keys():
        kn = jnp.concatenate(
            [nkv[:, 0:OWN, :].reshape(NZ * OWN, HD), jnp.zeros((NEW - NZ * OWN, HD), f32)], axis=0
        )
        vn = jnp.concatenate(
            [nkv[:, OWN : 2 * OWN, :].reshape(NZ * OWN, HD), jnp.zeros((NEW - NZ * OWN, HD), f32)], axis=0
        )
        high, low = split(kn)
        s = dot(queries(0), jnp.concatenate([high, high, low, jnp.zeros((NEW, HD), bf16)], axis=1), NT)
        row = lax.broadcasted_iota(jnp.int32, (R, NEW), 0)
        col = lax.broadcasted_iota(jnp.int32, (R, NEW), 1)
        token = (z * NX + (x + row // ROWS) % NX) * OWN + row % OWN
        key = ((col // OWN) * NX + x) * OWN + col % OWN
        s = jnp.where((key <= token) & (col < NZ * OWN), s, NEG)
        old = own_m[...]
        m = jnp.maximum(old, jnp.max(s, axis=1, keepdims=True))
        factor = jnp.exp2(old - m)
        high, low = split(vn)
        total, acc = fold(
            s, m, jnp.concatenate([high, low], axis=1), own_l[...] * factor, jnp.zeros((R, 2 * HD), f32)
        )
        finish(0, own_o[...] * factor + acc[:, :HD] + acc[:, HD:], m, total)

    def x_copy(p, i):
        dz, dx = CHUNKS[p][i]
        n = XSLOT[dz, dx]
        return remote(part.at[p, i], xin.at[n], x_s.at[n], x_r.at[n], ctx_at(0, dx))

    def z_copy(dz):
        n = ZSLOT[dz]
        return remote(zout.at[n], zin.at[n], z_s.at[n], z_r.at[n], ctx_at(dz, 0))

    arriving = {}

    def send(p):
        for i, pair in enumerate(CHUNKS[p]):
            if pair in XSLOT:
                arriving["x", pair] = x_copy(p, i)
                go(arriving["x", pair])

    def merge(pieces):
        tiles = [piece[ROWS:PIECE, :] for piece in pieces]
        peaks = [tile[0:1] for tile in tiles]
        top = functools.reduce(jnp.maximum, peaks)
        factors = [jnp.exp2(one - top) for one in peaks]
        total = functools.reduce(jnp.add, [f * tile[1:2] for f, tile in zip(factors, tiles)])
        pad = [jnp.zeros((1, HD), f32)] * (8 - len(factors))
        cols = jnp.concatenate(factors + pad, axis=0).T[0:ROWS]
        out = functools.reduce(
            jnp.add, [cols[:, i : i + 1] * piece[0:ROWS, :] for i, piece in enumerate(pieces)]
        )
        return out, jnp.concatenate([top, total, jnp.zeros((6, HD), f32)], axis=0)

    def merge_to(dst, pieces):
        out, tile = merge(pieces)
        dst[0:ROWS, :] = out
        dst[ROWS:PIECE, :] = tile

    def merge_tokens(pieces, dst):
        tiles = [piece[ROWS:PIECE, :] for piece in pieces]
        peaks = [tile[0:1] for tile in tiles]
        top = functools.reduce(jnp.maximum, peaks)
        factors = [jnp.exp2(one - top) for one in peaks]
        total = functools.reduce(jnp.add, [f * tile[1:2] for f, tile in zip(factors, tiles)])
        n = len(factors)
        pad = [jnp.zeros((1, HD), f32)] * (6 - n)
        cols = jnp.concatenate(factors + [top, total] + pad, axis=0).T[0:ROWS]
        otmp[...] = functools.reduce(
            jnp.add, [cols[:, i : i + 1] * piece[0:ROWS, :] for i, piece in enumerate(pieces)]
        )
        lane = lax.broadcasted_iota(jnp.int32, (ROWS, HD), 1)
        omax[...] = jnp.where(lane < HD // 2, cols[:, n : n + 1], cols[:, n + 1 : n + 2])
        for t in range(OWN):
            dst[t, 0:GROUP, :] = otmp[pl.ds(t, GROUP, stride=OWN), :]
            dst[t, GROUP : 2 * GROUP, :] = omax[pl.ds(t, GROUP, stride=OWN), :]

    def token_copies(n, dz):
        copies = []
        for k in range(0 if dz else 1, KVH):
            there = (g + k) % KVH
            dev = {**ctx_at(dz, 0), "kvh": there} if dz else {"kvh": there}
            copies.append(remote(osend.at[n, there], oin.at[n, g], o_s.at[n, k], o_r.at[n, k], dev))
        for copy in copies:
            copy.start()
        return copies

    where = {pair: (p, i) for p, chunk in enumerate(CHUNKS) for i, pair in enumerate(chunk)}

    def merge_x(dz):
        pieces = [part.at[where[dz, 0]]]
        for dx in (1, 2, 3):
            arriving["x", (dz, dx)].wait_recv()
            pieces.append(xin.at[XSLOT[dz, dx]])
        merge_to(zout.at[ZSLOT[dz]], pieces)

    def send_z(*dzs):
        for dz in dzs:
            arriving["z", dz] = z_copy(dz)
            go(arriving["z", dz])

    def z_wait(dz):
        arriving["z", dz].wait_recv()
        return zin.at[ZSLOT[dz]]

    def x_wait(pair):
        arriving["x", pair].wait_recv()
        return xin.at[XSLOT[pair]]

    new_copies = [
        remote(nkv.at[z], nkv.at[z], n_s.at[k - 1], n_r.at[k - 1], ctx_at(k, 0)) for k in range(1, NZ)
    ]

    for i in range(4):
        prep_part(i)
    pl.semaphore_wait(barrier, len(partners))
    own = [own_copy(dx) for dx in (1, 2, 3)]
    for copy in own:
        go(copy)
    far = {dz: far_copy(dz) for dz in (4, 3, -3)}
    for copy in far.values():
        go(copy)
    near = {(dz, dx): near_copy(dz, dx) for dz in (1, -1) for dx in range(NX)}
    go(near[1, 0])
    go(near[-1, 0])
    for dx in (1, 3, 2):
        own[dx - 1].wait_recv()
        go(near[1, dx])
        go(near[-1, dx])
    rows = {dz: row_copy(dz) for dz in (2, -2)}
    phase(0, None)
    phase(None, 0)
    passed = {(dz, dx): pass_copy(dz, dx) for dz in far for dx in (1, 2, 3)}
    for dz in far:
        far[dz].wait_recv()
        for dx in (1, 2, 3):
            go(passed[dz, dx])
    for dx in range(NX):
        near[1, dx].wait_recv()
    go(rows[2])
    phase(1, None)
    for dx in range(NX):
        near[-1, dx].wait_recv()
    go(rows[-2])
    for copy in new_copies:
        go(copy)
    phase(2, 1)
    send(1)

    def wait_passed(dz):
        for dx in (1, 2, 3):
            passed[dz, dx].wait_recv()

    wait_passed(4)
    phase(3, 2)
    send(2)
    wait_passed(3)
    phase(4, 3)
    send(3)
    for copy in new_copies:
        copy.wait_recv()
    new_keys()
    send(0)
    wait_passed(-3)
    merge_x(1)
    phase(5, 4)
    send(4)
    send_z(1)
    rows[2].wait_recv()
    merge_x(-1)
    merge_x(4)
    phase(6, 5)
    send(5)
    send_z(-1, 4)
    rows[-2].wait_recv()
    merge_x(3)
    phase(7, 6)
    send(6)
    send_z(3)
    phase(None, 7)
    send(7)
    merge_x(-3)
    send_z(-3)
    pieces = [part.at[0, 0]] + [x_wait((0, dx)) for dx in (1, 2, 3)] + [z_wait(dz) for dz in (1, -1, 4)]
    merge_to(acc1, pieces)
    def pieces_x(dz):
        return [part.at[where[dz, 0]]] + [x_wait((dz, dx)) for dx in (1, 2, 3)]

    merge_tokens(pieces_x(2), osend.at[1])
    o_copies = token_copies(1, 2)
    merge_tokens(pieces_x(-2), osend.at[2])
    o_copies += token_copies(2, -2)
    merge_tokens([acc1] + [z_wait(dz) for dz in (3, -3)], osend.at[0])
    o_copies += token_copies(0, 0)
    oin[0, g] = osend[0, g]
    for copy in sent:
        copy.wait_send()
    for copy in o_copies:
        copy.wait_recv()
    outs = [oin[n, :, 0:GROUP, :].reshape(HQ, HD) for n in range(3)]
    tiles = [oin[n, :, GROUP : 2 * GROUP, :].reshape(HQ, HD) for n in range(3)]
    peaks = [tile[:, 0:1] for tile in tiles]
    top = functools.reduce(jnp.maximum, peaks)
    factors = [jnp.exp2(one - top) for one in peaks]
    total = functools.reduce(jnp.add, [f * tile[:, HD // 2 : HD // 2 + 1] for f, tile in zip(factors, tiles)])
    o_ref[...] = functools.reduce(jnp.add, [f * out for f, out in zip(factors, outs)]) / total
    for copy in o_copies:
        copy.wait_send()


def per_device(queries, cache_keys, cache_values, new_keys, new_values, block_lengths):
    vmem = pl.BlockSpec(memory_space=pltpu.VMEM)
    hbm = pl.BlockSpec(memory_space=pl.ANY)
    dma = pltpu.SemaphoreType.DMA
    out = pl.pallas_call(
        kernel,
        out_shape=jax.ShapeDtypeStruct((HQ, HD), f32),
        in_specs=[hbm, hbm, hbm, hbm, hbm, pl.BlockSpec(memory_space=pltpu.SMEM)],
        out_specs=vmem,
        scratch_shapes=[
            pltpu.VMEM((OWN, GROUP * HD), f32),
            pltpu.VMEM((BLK, HD), f32),
            pltpu.VMEM((BLK, HD), f32),
            pltpu.VMEM((BLK, 4 * HD), bf16),
            pltpu.VMEM((BLK, 2 * HD), bf16),
            pltpu.VMEM((NZ, NX, ROWS, HD), f32),
            pltpu.VMEM((NZ, 2 * OWN, HD), f32),
            pltpu.VMEM((R, BLK), f32),
            pltpu.VMEM((2, R, HD), f32),
            pltpu.VMEM((R, HD), f32),
            pltpu.VMEM((R, HD), f32),
            pltpu.VMEM((R, HD), f32),
            pltpu.VMEM((len(CHUNKS), NX, PIECE, HD), f32),
            pltpu.VMEM((len(XSLOT), PIECE, HD), f32),
            pltpu.VMEM((len(ZSLOT), PIECE, HD), f32),
            pltpu.VMEM((len(ZSLOT), PIECE, HD), f32),
            pltpu.VMEM((PIECE, HD), f32),
            pltpu.VMEM((ROWS, HD), f32),
            pltpu.VMEM((ROWS, HD), f32),
            pltpu.VMEM((3, OWN, 2 * GROUP, HD), f32),
            pltpu.VMEM((3, KVH, 2 * GROUP, HD), f32),
            dma((3,)),
            dma((4,)),
            dma((4,)),
            dma((NZ, NX)),
            dma((NZ, NX)),
            dma((NZ - 1,)),
            dma((NZ - 1,)),
            dma((len(XSLOT),)),
            dma((len(XSLOT),)),
            dma((len(ZSLOT),)),
            dma((len(ZSLOT),)),
            dma((3, KVH)),
            dma((3, KVH)),
        ],
        compiler_params=pltpu.CompilerParams(
            collective_id=0, has_side_effects=True, vmem_limit_bytes=56 * 1024 * 1024
        ),
        cost_estimate=pl.CostEstimate(
            flops=2 * 2 * 2048 * BLK * HD * 3, bytes_accessed=5 * 1024 * 1024, transcendentals=2048 * BLK
        ),
    )(queries, cache_keys, cache_values, new_keys, new_values, block_lengths)
    return out.reshape(1, HQ * HD)


def solution(mesh):
    in_specs = (P("ctx", "kvh"),) * 5 + (P("ctx"),)
    return jax.shard_map(
        per_device, mesh=mesh, in_specs=in_specs, out_specs=P(("ctx", "kvh"), None), check_vma=False
    )
```

```python
import functools
import math

import jax
import jax.numpy as jnp
from jax import lax
from jax.experimental import pallas as pl
from jax.experimental.pallas import tpu as pltpu
from jax.sharding import PartitionSpec as P

HQ = 64
KVH = 8
HD = 128
GROUP = HQ // KVH
NZ, NX = 8, 4
BLK = 4096
OWN = 8
ROWS = OWN * GROUP
R = NX * ROWS
PIECE = ROWS + 8
NEW = 128
T = 512
SCALE = math.log2(math.e) / math.sqrt(HD)
NEG = -1e30
MESH = pl.DeviceIdType.MESH
bf16, f32 = jnp.bfloat16, jnp.float32
NT = (((1,), (1,)), ((), ()))
NN = (((1,), (0,)), ((), ()))


def dot(a, b, dims):
    return lax.dot_general(a, b, dims, preferred_element_type=f32)


def split(x):
    high = x.astype(bf16)
    return high, (x - high.astype(f32)).astype(bf16)


ORDER = [0, 1, -1, 4, 3, -3, 2, -2]
CHUNKS = [[(dz, i) for i in range(NX)] for dz in ORDER]
FAR = ORDER[1:]
XSLOT = {pair: i for i, pair in enumerate([(dz, dx) for dz in ORDER for dx in (1, 2, 3)])}
ZSLOT = {dz: i for i, dz in enumerate(FAR)}


def kernel(
    q_ref, k_ref, v_ref, nk_ref, nv_ref, len_ref, o_ref,
    qin, kbuf, vbuf, kc, vc, qbuf, nkv, sbuf, mbuf, own_o, own_l, own_m, part, xin, zout, zin, acc1,
    otmp, omax, osend, oin,
    in_s, ksem, vsem, q_s, q_r, n_s, n_r, x_s, x_r, z_s, z_r, o_s, o_r,
):
    c = lax.axis_index("ctx")
    g = lax.axis_index("kvh")
    z, x = c // NX, c % NX

    def ctx_at(dz, dx):
        return {"ctx": ((z + dz + NZ) % NZ) * NX + (x + dx + NX) % NX}

    def remote(src, dst, ssem, rsem, dev):
        return pltpu.make_async_remote_copy(
            src_ref=src, dst_ref=dst, send_sem=ssem, recv_sem=rsem, device_id=dev, device_id_type=MESH
        )

    offsets = {(0, k) for k in (1, 2, 3)} | {(k, 0) for k in range(1, NZ)}
    partners = [ctx_at(*pair) for pair in sorted(offsets, key=lambda pair: (min(pair[0], NZ - pair[0]), pair))]
    partners += [{"kvh": (g + k) % KVH} for k in range(1, KVH)]
    partners += [{**ctx_at(dz, 0), "kvh": (g + k) % KVH} for dz in (2, -2) for k in range(1, KVH)]
    barrier = pltpu.get_barrier_semaphore()
    for dev in partners:
        pl.semaphore_signal(barrier, inc=1, device_id=dev, device_id_type=MESH)

    firsts = [
        pltpu.make_async_copy(q_ref, qin, in_s.at[0]),
        pltpu.make_async_copy(nk_ref, nkv.at[z, 0:OWN], in_s.at[1]),
        pltpu.make_async_copy(nv_ref, nkv.at[z, OWN : 2 * OWN], in_s.at[2]),
    ]
    for copy in firsts:
        copy.start()
    loads = []
    for i in range(4):
        rows = pl.ds(i * 1024, 1024)
        loads.append(
            (
                pltpu.make_async_copy(k_ref.at[rows], kbuf.at[rows], ksem.at[i]),
                pltpu.make_async_copy(v_ref.at[rows], vbuf.at[rows], vsem.at[i]),
            )
        )
    for one, two in loads:
        one.start()
        two.start()

    for copy in firsts:
        copy.wait()
    for h in range(GROUP):
        qbuf[z, x, h * OWN : (h + 1) * OWN, :] = qin[:, h * HD : (h + 1) * HD]

    sent = []

    def go(copy):
        copy.start()
        sent.append(copy)

    def own_copy(dx):
        return remote(qbuf.at[z, x], qbuf.at[z, x], q_s.at[0, dx], q_r.at[0, dx], ctx_at(0, -dx))

    def near_copy(dz, dx):
        block = qbuf.at[z, (x + dx) % NX]
        return remote(block, block, q_s.at[dz % NZ, dx], q_r.at[dz % NZ, dx], ctx_at(-dz, 0))

    def row_copy(dz):
        side = 1 if dz > 0 else -1
        row = qbuf.at[(z + dz - side + NZ) % NZ]
        return remote(row, row, q_s.at[dz % NZ, 0], q_r.at[dz % NZ, 0], ctx_at(-side, 0))

    def far_copy(dz):
        return remote(qbuf.at[z, x], qbuf.at[z, x], q_s.at[dz % NZ, 0], q_r.at[dz % NZ, 0], ctx_at(-dz, 0))

    def pass_copy(dz, dx):
        block = qbuf.at[(z + dz + NZ) % NZ, x]
        return remote(block, block, q_s.at[dz % NZ, dx], q_r.at[dz % NZ, dx], ctx_at(0, -dx))

    filled = len_ref[0]

    def prep(i, _):
        r = pl.ds(pl.multiple_of(i * 256, 256), 256)
        high, low = split(kbuf[r, :])
        kc[r, 0:128] = high
        kc[r, 128:256] = high
        kc[r, 256:384] = low
        pos = i * 256 + lax.broadcasted_iota(jnp.int32, (256, 128), 0)
        lane = lax.broadcasted_iota(jnp.int32, (256, 128), 1)
        kc[r, 384:512] = jnp.where((lane == 0) & (pos >= filled), NEG, 0.0).astype(bf16)
        high, low = split(vbuf[r, :])
        vc[r, 0:128] = high
        vc[r, 128:256] = low
        return 0

    def prep_part(i):
        loads[i][0].wait()
        loads[i][1].wait()
        lax.fori_loop(i * 4, i * 4 + 4, prep, 0)

    def queries(p):
        rows = [qbuf[(z + dz + NZ) % NZ, (x + dx) % NX] for dz, dx in CHUNKS[p]]
        high, low = split(jnp.concatenate(rows, axis=0) * SCALE)
        lane = lax.broadcasted_iota(jnp.int32, (R, HD), 1)
        return jnp.concatenate([high, low, high, jnp.where(lane == 0, 1.0, 0.0).astype(bf16)], axis=1)

    def fold(s, m, vt, total, acc):
        width = s.shape[1]
        w = jnp.exp2(s - jnp.concatenate([m] * (width // 128), axis=1))
        for i in range(width // 128):
            total = total + w[:, i * 128 : (i + 1) * 128]
        high, low = split(w)
        return total, acc + dot(high, vt, NN) + dot(low, vt, NN)

    def finish(p, out, m, total):
        total = jnp.sum(total, axis=1, keepdims=True)
        lane = lax.broadcasted_iota(jnp.int32, (R, HD), 1)
        both = jnp.where(lane == 0, m, jnp.where(lane == 1, total, 0.0))
        for i in range(NX):
            part[p, i, 0:ROWS, :] = out[i * ROWS : (i + 1) * ROWS]
        for i in range(NX // 2):
            tile = both[i * 128 : (i + 1) * 128].T[0:8]
            part[p, 2 * i, ROWS:PIECE, :] = tile
            part[p, 2 * i + 1, ROWS:PIECE, :] = jnp.concatenate([tile[:, 64:], tile[:, :64]], axis=1)

    def phase(score, attend):
        if score is not None:
            qc = queries(score)
            mx = None
        if attend is not None:
            m = mbuf[attend % 2]
            total = jnp.zeros((R, HD), f32)
            acc = jnp.zeros((R, 2 * HD), f32)
        for j in range(BLK // T):
            t = slice(j * T, (j + 1) * T)
            if attend is not None:
                total, acc = fold(sbuf[:, t], m, vc[t, :], total, acc)
            if score is not None:
                s = dot(qc, kc[t, :], NT)
                sbuf[:, t] = s
                for i in range(T // 128):
                    one = s[:, i * 128 : (i + 1) * 128]
                    mx = one if mx is None else jnp.maximum(mx, one)
        if attend is not None:
            out = acc[:, :HD] + acc[:, HD:]
            if attend == 0:
                own_o[...] = out
                own_l[...] = total
                own_m[...] = m
            else:
                finish(attend, out, m, total)
        if score is not None:
            mbuf[score % 2] = jnp.broadcast_to(jnp.max(mx, axis=1, keepdims=True), (R, HD))

    def new_keys():
        kn = jnp.concatenate(
            [nkv[:, 0:OWN, :].reshape(NZ * OWN, HD), jnp.zeros((NEW - NZ * OWN, HD), f32)], axis=0
        )
        vn = jnp.concatenate(
            [nkv[:, OWN : 2 * OWN, :].reshape(NZ * OWN, HD), jnp.zeros((NEW - NZ * OWN, HD), f32)], axis=0
        )
        high, low = split(kn)
        s = dot(queries(0), jnp.concatenate([high, high, low, jnp.zeros((NEW, HD), bf16)], axis=1), NT)
        row = lax.broadcasted_iota(jnp.int32, (R, NEW), 0)
        col = lax.broadcasted_iota(jnp.int32, (R, NEW), 1)
        token = (z * NX + (x + row // ROWS) % NX) * OWN + row % OWN
        key = ((col // OWN) * NX + x) * OWN + col % OWN
        s = jnp.where((key <= token) & (col < NZ * OWN), s, NEG)
        old = own_m[...]
        m = jnp.maximum(old, jnp.max(s, axis=1, keepdims=True))
        factor = jnp.exp2(old - m)
        high, low = split(vn)
        total, acc = fold(
            s, m, jnp.concatenate([high, low], axis=1), own_l[...] * factor, jnp.zeros((R, 2 * HD), f32)
        )
        finish(0, own_o[...] * factor + acc[:, :HD] + acc[:, HD:], m, total)

    def x_copy(p, i):
        dz, dx = CHUNKS[p][i]
        n = XSLOT[dz, dx]
        return remote(part.at[p, i], xin.at[n], x_s.at[n], x_r.at[n], ctx_at(0, dx))

    def z_copy(dz):
        n = ZSLOT[dz]
        return remote(zout.at[n], zin.at[n], z_s.at[n], z_r.at[n], ctx_at(dz, 0))

    arriving = {}

    def send(p):
        for i, pair in enumerate(CHUNKS[p]):
            if pair in XSLOT:
                arriving["x", pair] = x_copy(p, i)
                go(arriving["x", pair])

    def merge(pieces):
        tiles = [piece[ROWS:PIECE, :] for piece in pieces]
        peaks = [tile[0:1] for tile in tiles]
        top = functools.reduce(jnp.maximum, peaks)
        factors = [jnp.exp2(one - top) for one in peaks]
        total = functools.reduce(jnp.add, [f * tile[1:2] for f, tile in zip(factors, tiles)])
        pad = [jnp.zeros((1, HD), f32)] * (8 - len(factors))
        cols = jnp.concatenate(factors + pad, axis=0).T[0:ROWS]
        out = functools.reduce(
            jnp.add, [cols[:, i : i + 1] * piece[0:ROWS, :] for i, piece in enumerate(pieces)]
        )
        return out, jnp.concatenate([top, total, jnp.zeros((6, HD), f32)], axis=0)

    def merge_to(dst, pieces):
        out, tile = merge(pieces)
        dst[0:ROWS, :] = out
        dst[ROWS:PIECE, :] = tile

    def merge_tokens(pieces, dst):
        tiles = [piece[ROWS:PIECE, :] for piece in pieces]
        peaks = [tile[0:1] for tile in tiles]
        top = functools.reduce(jnp.maximum, peaks)
        factors = [jnp.exp2(one - top) for one in peaks]
        total = functools.reduce(jnp.add, [f * tile[1:2] for f, tile in zip(factors, tiles)])
        n = len(factors)
        pad = [jnp.zeros((1, HD), f32)] * (6 - n)
        cols = jnp.concatenate(factors + [top, total] + pad, axis=0).T[0:ROWS]
        otmp[...] = functools.reduce(
            jnp.add, [cols[:, i : i + 1] * piece[0:ROWS, :] for i, piece in enumerate(pieces)]
        )
        lane = lax.broadcasted_iota(jnp.int32, (ROWS, HD), 1)
        omax[...] = jnp.where(lane < HD // 2, cols[:, n : n + 1], cols[:, n + 1 : n + 2])
        for t in range(OWN):
            dst[t, 0:GROUP, :] = otmp[pl.ds(t, GROUP, stride=OWN), :]
            dst[t, GROUP : 2 * GROUP, :] = omax[pl.ds(t, GROUP, stride=OWN), :]

    def token_copies(n, dz):
        copies = []
        for k in range(0 if dz else 1, KVH):
            there = (g + k) % KVH
            dev = {**ctx_at(dz, 0), "kvh": there} if dz else {"kvh": there}
            copies.append(remote(osend.at[n, there], oin.at[n, g], o_s.at[n, k], o_r.at[n, k], dev))
        for copy in copies:
            copy.start()
        return copies

    where = {pair: (p, i) for p, chunk in enumerate(CHUNKS) for i, pair in enumerate(chunk)}

    def wait_x(*dzs):
        for dz in dzs:
            for dx in (1, 2, 3):
                arriving["x", (dz, dx)].wait_recv()

    def merge_x(dz):
        pieces = [part.at[where[dz, 0]]]
        for dx in (1, 2, 3):
            pieces.append(xin.at[XSLOT[dz, dx]])
        merge_to(zout.at[ZSLOT[dz]], pieces)

    def send_z(*dzs):
        for dz in dzs:
            arriving["z", dz] = z_copy(dz)
            go(arriving["z", dz])

    def z_wait(dz):
        arriving["z", dz].wait_recv()
        return zin.at[ZSLOT[dz]]

    def x_wait(pair):
        arriving["x", pair].wait_recv()
        return xin.at[XSLOT[pair]]

    new_copies = [
        remote(nkv.at[z], nkv.at[z], n_s.at[k - 1], n_r.at[k - 1], ctx_at(k, 0)) for k in range(1, NZ)
    ]

    for i in range(4):
        prep_part(i)
    pl.semaphore_wait(barrier, len(partners))
    own = [own_copy(dx) for dx in (1, 2, 3)]
    for copy in own:
        go(copy)
    far = {dz: far_copy(dz) for dz in (4, 3, -3)}
    for copy in far.values():
        go(copy)
    near = {(dz, dx): near_copy(dz, dx) for dz in (1, -1) for dx in range(NX)}
    go(near[1, 0])
    go(near[-1, 0])
    for dx in (1, 3, 2):
        own[dx - 1].wait_recv()
        go(near[1, dx])
        go(near[-1, dx])
    rows = {dz: row_copy(dz) for dz in (2, -2)}
    phase(0, None)
    phase(None, 0)
    passed = {(dz, dx): pass_copy(dz, dx) for dz in far for dx in (1, 2, 3)}
    for dz in far:
        far[dz].wait_recv()
        for dx in (1, 2, 3):
            go(passed[dz, dx])
    for dx in range(NX):
        near[1, dx].wait_recv()
    go(rows[2])
    phase(1, None)
    for dx in range(NX):
        near[-1, dx].wait_recv()
    go(rows[-2])
    for copy in new_copies:
        go(copy)
    phase(2, 1)
    send(1)

    def wait_passed(dz):
        for dx in (1, 2, 3):
            passed[dz, dx].wait_recv()

    wait_passed(4)
    phase(3, 2)
    send(2)
    wait_passed(3)
    phase(4, 3)
    send(3)
    for copy in new_copies:
        copy.wait_recv()
    wait_passed(-3)
    wait_x(1)
    new_keys()
    merge_x(1)
    phase(5, 4)
    send(4)
    send(0)
    send_z(1)
    rows[2].wait_recv()
    wait_x(-1, 4)
    merge_x(-1)
    merge_x(4)
    phase(6, 5)
    send(5)
    send_z(-1, 4)
    rows[-2].wait_recv()
    wait_x(3)
    merge_x(3)
    phase(7, 6)
    send(6)
    send_z(3)
    phase(None, 7)
    send(7)
    wait_x(-3)
    merge_x(-3)
    send_z(-3)
    pieces = [part.at[0, 0]] + [x_wait((0, dx)) for dx in (1, 2, 3)] + [z_wait(dz) for dz in (1, -1, 4)]
    merge_to(acc1, pieces)
    def pieces_x(dz):
        return [part.at[where[dz, 0]]] + [x_wait((dz, dx)) for dx in (1, 2, 3)]

    merge_tokens(pieces_x(2), osend.at[1])
    o_copies = token_copies(1, 2)
    merge_tokens(pieces_x(-2), osend.at[2])
    o_copies += token_copies(2, -2)
    merge_tokens([acc1] + [z_wait(dz) for dz in (3, -3)], osend.at[0])
    o_copies += token_copies(0, 0)
    oin[0, g] = osend[0, g]
    for copy in sent:
        copy.wait_send()
    for copy in o_copies:
        copy.wait_recv()
    outs = [oin[n, :, 0:GROUP, :].reshape(HQ, HD) for n in range(3)]
    tiles = [oin[n, :, GROUP : 2 * GROUP, :].reshape(HQ, HD) for n in range(3)]
    peaks = [tile[:, 0:1] for tile in tiles]
    top = functools.reduce(jnp.maximum, peaks)
    factors = [jnp.exp2(one - top) for one in peaks]
    total = functools.reduce(jnp.add, [f * tile[:, HD // 2 : HD // 2 + 1] for f, tile in zip(factors, tiles)])
    o_ref[...] = functools.reduce(jnp.add, [f * out for f, out in zip(factors, outs)]) / total
    for copy in o_copies:
        copy.wait_send()


def per_device(queries, cache_keys, cache_values, new_keys, new_values, block_lengths):
    vmem = pl.BlockSpec(memory_space=pltpu.VMEM)
    hbm = pl.BlockSpec(memory_space=pl.ANY)
    dma = pltpu.SemaphoreType.DMA
    out = pl.pallas_call(
        kernel,
        out_shape=jax.ShapeDtypeStruct((HQ, HD), f32),
        in_specs=[hbm, hbm, hbm, hbm, hbm, pl.BlockSpec(memory_space=pltpu.SMEM)],
        out_specs=vmem,
        scratch_shapes=[
            pltpu.VMEM((OWN, GROUP * HD), f32),
            pltpu.VMEM((BLK, HD), f32),
            pltpu.VMEM((BLK, HD), f32),
            pltpu.VMEM((BLK, 4 * HD), bf16),
            pltpu.VMEM((BLK, 2 * HD), bf16),
            pltpu.VMEM((NZ, NX, ROWS, HD), f32),
            pltpu.VMEM((NZ, 2 * OWN, HD), f32),
            pltpu.VMEM((R, BLK), f32),
            pltpu.VMEM((2, R, HD), f32),
            pltpu.VMEM((R, HD), f32),
            pltpu.VMEM((R, HD), f32),
            pltpu.VMEM((R, HD), f32),
            pltpu.VMEM((len(CHUNKS), NX, PIECE, HD), f32),
            pltpu.VMEM((len(XSLOT), PIECE, HD), f32),
            pltpu.VMEM((len(ZSLOT), PIECE, HD), f32),
            pltpu.VMEM((len(ZSLOT), PIECE, HD), f32),
            pltpu.VMEM((PIECE, HD), f32),
            pltpu.VMEM((ROWS, HD), f32),
            pltpu.VMEM((ROWS, HD), f32),
            pltpu.VMEM((3, OWN, 2 * GROUP, HD), f32),
            pltpu.VMEM((3, KVH, 2 * GROUP, HD), f32),
            dma((3,)),
            dma((4,)),
            dma((4,)),
            dma((NZ, NX)),
            dma((NZ, NX)),
            dma((NZ - 1,)),
            dma((NZ - 1,)),
            dma((len(XSLOT),)),
            dma((len(XSLOT),)),
            dma((len(ZSLOT),)),
            dma((len(ZSLOT),)),
            dma((3, KVH)),
            dma((3, KVH)),
        ],
        compiler_params=pltpu.CompilerParams(
            collective_id=0, has_side_effects=True, vmem_limit_bytes=56 * 1024 * 1024
        ),
        cost_estimate=pl.CostEstimate(
            flops=2 * 2 * 2048 * BLK * HD * 3, bytes_accessed=5 * 1024 * 1024, transcendentals=2048 * BLK
        ),
    )(queries, cache_keys, cache_values, new_keys, new_values, block_lengths)
    return out.reshape(1, HQ * HD)


def solution(mesh):
    in_specs = (P("ctx", "kvh"),) * 5 + (P("ctx"),)
    return jax.shard_map(
        per_device, mesh=mesh, in_specs=in_specs, out_specs=P(("ctx", "kvh"), None), check_vma=False
    )
```

```python
import functools
import math

import jax
import jax.numpy as jnp
from jax import lax
from jax.experimental import pallas as pl
from jax.experimental.pallas import tpu as pltpu
from jax.sharding import PartitionSpec as P

HQ = 64
KVH = 8
HD = 128
GROUP = HQ // KVH
NZ, NX = 8, 4
BLK = 4096
OWN = 8
ROWS = OWN * GROUP
R = NX * ROWS
PIECE = ROWS + 8
NEW = 128
T = 512
SCALE = math.log2(math.e) / math.sqrt(HD)
NEG = -1e30
MESH = pl.DeviceIdType.MESH
bf16, f32 = jnp.bfloat16, jnp.float32
NT = (((1,), (1,)), ((), ()))
NN = (((1,), (0,)), ((), ()))


def dot(a, b, dims):
    return lax.dot_general(a, b, dims, preferred_element_type=f32)


def split(x):
    high = x.astype(bf16)
    return high, (x - high.astype(f32)).astype(bf16)


ORDER = [0, 1, -1, 4, 3, -3, 2, -2]
CHUNKS = [[(dz, i) for i in range(NX)] for dz in ORDER]
FAR = ORDER[1:]
XSLOT = {pair: i for i, pair in enumerate([(dz, dx) for dz in ORDER for dx in (1, 2, 3)])}
ZSLOT = {dz: i for i, dz in enumerate(FAR)}


def kernel(
    q_ref, k_ref, v_ref, nk_ref, nv_ref, len_ref, o_ref,
    qin, kbuf, vbuf, kc, vc, qbuf, nkv, sbuf, mbuf, own_o, own_l, own_m, part, xin, zout, zin, acc1,
    otmp, omax, osend, oin,
    in_s, ksem, vsem, q_s, q_r, n_s, n_r, x_s, x_r, z_s, z_r, o_s, o_r,
):
    c = lax.axis_index("ctx")
    g = lax.axis_index("kvh")
    z, x = c // NX, c % NX

    def ctx_at(dz, dx):
        return {"ctx": ((z + dz + NZ) % NZ) * NX + (x + dx + NX) % NX}

    def remote(src, dst, ssem, rsem, dev):
        return pltpu.make_async_remote_copy(
            src_ref=src, dst_ref=dst, send_sem=ssem, recv_sem=rsem, device_id=dev, device_id_type=MESH
        )

    offsets = {(0, k) for k in (1, 2, 3)} | {(k, 0) for k in range(1, NZ)}
    partners = [ctx_at(*pair) for pair in sorted(offsets, key=lambda pair: (min(pair[0], NZ - pair[0]), pair))]
    partners += [{"kvh": (g + k) % KVH} for k in range(1, KVH)]
    partners += [{**ctx_at(dz, 0), "kvh": (g + k) % KVH} for dz in (2, -2) for k in range(1, KVH)]
    barrier = pltpu.get_barrier_semaphore()
    for dev in partners:
        pl.semaphore_signal(barrier, inc=1, device_id=dev, device_id_type=MESH)

    firsts = [
        pltpu.make_async_copy(q_ref, qin, in_s.at[0]),
        pltpu.make_async_copy(nk_ref, nkv.at[z, 0:OWN], in_s.at[1]),
        pltpu.make_async_copy(nv_ref, nkv.at[z, OWN : 2 * OWN], in_s.at[2]),
    ]
    for copy in firsts:
        copy.start()
    loads = []
    for i in range(4):
        rows = pl.ds(i * 1024, 1024)
        loads.append(
            (
                pltpu.make_async_copy(k_ref.at[rows], kbuf.at[rows], ksem.at[i]),
                pltpu.make_async_copy(v_ref.at[rows], vbuf.at[rows], vsem.at[i]),
            )
        )
    for one, two in loads:
        one.start()
        two.start()

    for copy in firsts:
        copy.wait()
    for h in range(GROUP):
        qbuf[z, x, h * OWN : (h + 1) * OWN, :] = qin[:, h * HD : (h + 1) * HD]

    sent = []

    def go(copy):
        copy.start()
        sent.append(copy)

    def own_copy(dx):
        return remote(qbuf.at[z, x], qbuf.at[z, x], q_s.at[0, dx], q_r.at[0, dx], ctx_at(0, -dx))

    def near_copy(dz, dx):
        block = qbuf.at[z, (x + dx) % NX]
        return remote(block, block, q_s.at[dz % NZ, dx], q_r.at[dz % NZ, dx], ctx_at(-dz, 0))

    def row_copy(dz):
        side = 1 if dz > 0 else -1
        row = qbuf.at[(z + dz - side + NZ) % NZ]
        return remote(row, row, q_s.at[dz % NZ, 0], q_r.at[dz % NZ, 0], ctx_at(-side, 0))

    def far_copy(dz):
        return remote(qbuf.at[z, x], qbuf.at[z, x], q_s.at[dz % NZ, 0], q_r.at[dz % NZ, 0], ctx_at(-dz, 0))

    def pass_copy(dz, dx):
        block = qbuf.at[(z + dz + NZ) % NZ, x]
        return remote(block, block, q_s.at[dz % NZ, dx], q_r.at[dz % NZ, dx], ctx_at(0, -dx))

    filled = len_ref[0]

    def prep(i, _):
        r = pl.ds(pl.multiple_of(i * 256, 256), 256)
        high, low = split(kbuf[r, :])
        kc[r, 0:128] = high
        kc[r, 128:256] = high
        kc[r, 256:384] = low
        pos = i * 256 + lax.broadcasted_iota(jnp.int32, (256, 128), 0)
        lane = lax.broadcasted_iota(jnp.int32, (256, 128), 1)
        kc[r, 384:512] = jnp.where((lane == 0) & (pos >= filled), NEG, 0.0).astype(bf16)
        high, low = split(vbuf[r, :])
        vc[r, 0:128] = high
        vc[r, 128:256] = low
        return 0

    def prep_part(i):
        loads[i][0].wait()
        loads[i][1].wait()
        lax.fori_loop(i * 4, i * 4 + 4, prep, 0)

    def queries(p):
        rows = [qbuf[(z + dz + NZ) % NZ, (x + dx) % NX] for dz, dx in CHUNKS[p]]
        high, low = split(jnp.concatenate(rows, axis=0) * SCALE)
        lane = lax.broadcasted_iota(jnp.int32, (R, HD), 1)
        return jnp.concatenate([high, low, high, jnp.where(lane == 0, 1.0, 0.0).astype(bf16)], axis=1)

    def fold(s, m, vt, total, acc):
        width = s.shape[1]
        w = jnp.exp2(s - jnp.concatenate([m] * (width // 128), axis=1))
        for i in range(width // 128):
            total = total + w[:, i * 128 : (i + 1) * 128]
        high, low = split(w)
        return total, acc + dot(high, vt, NN) + dot(low, vt, NN)

    def finish(p, out, m, total):
        total = jnp.sum(total, axis=1, keepdims=True)
        lane = lax.broadcasted_iota(jnp.int32, (R, HD), 1)
        both = jnp.where(lane == 0, m, jnp.where(lane == 1, total, 0.0))
        for i in range(NX):
            part[p, i, 0:ROWS, :] = out[i * ROWS : (i + 1) * ROWS]
        for i in range(NX // 2):
            tile = both[i * 128 : (i + 1) * 128].T[0:8]
            part[p, 2 * i, ROWS:PIECE, :] = tile
            part[p, 2 * i + 1, ROWS:PIECE, :] = jnp.concatenate([tile[:, 64:], tile[:, :64]], axis=1)

    def phase(score, attend):
        if score is not None:
            qc = queries(score)
            mx = None
        if attend is not None:
            m = mbuf[attend % 2]
            total = jnp.zeros((R, HD), f32)
            acc = jnp.zeros((R, 2 * HD), f32)
        for j in range(BLK // T):
            t = slice(j * T, (j + 1) * T)
            if attend is not None:
                total, acc = fold(sbuf[:, t], m, vc[t, :], total, acc)
            if score is not None:
                s = dot(qc, kc[t, :], NT)
                sbuf[:, t] = s
                for i in range(T // 128):
                    one = s[:, i * 128 : (i + 1) * 128]
                    mx = one if mx is None else jnp.maximum(mx, one)
        if attend is not None:
            out = acc[:, :HD] + acc[:, HD:]
            if attend == 0:
                own_o[...] = out
                own_l[...] = total
                own_m[...] = m
            else:
                finish(attend, out, m, total)
        if score is not None:
            mbuf[score % 2] = jnp.broadcast_to(jnp.max(mx, axis=1, keepdims=True), (R, HD))

    def new_keys():
        kn = jnp.concatenate(
            [nkv[:, 0:OWN, :].reshape(NZ * OWN, HD), jnp.zeros((NEW - NZ * OWN, HD), f32)], axis=0
        )
        vn = jnp.concatenate(
            [nkv[:, OWN : 2 * OWN, :].reshape(NZ * OWN, HD), jnp.zeros((NEW - NZ * OWN, HD), f32)], axis=0
        )
        high, low = split(kn)
        s = dot(queries(0), jnp.concatenate([high, high, low, jnp.zeros((NEW, HD), bf16)], axis=1), NT)
        row = lax.broadcasted_iota(jnp.int32, (R, NEW), 0)
        col = lax.broadcasted_iota(jnp.int32, (R, NEW), 1)
        token = (z * NX + (x + row // ROWS) % NX) * OWN + row % OWN
        key = ((col // OWN) * NX + x) * OWN + col % OWN
        s = jnp.where((key <= token) & (col < NZ * OWN), s, NEG)
        old = own_m[...]
        m = jnp.maximum(old, jnp.max(s, axis=1, keepdims=True))
        factor = jnp.exp2(old - m)
        high, low = split(vn)
        total, acc = fold(
            s, m, jnp.concatenate([high, low], axis=1), own_l[...] * factor, jnp.zeros((R, 2 * HD), f32)
        )
        finish(0, own_o[...] * factor + acc[:, :HD] + acc[:, HD:], m, total)

    def x_copy(p, i):
        dz, dx = CHUNKS[p][i]
        n = XSLOT[dz, dx]
        return remote(part.at[p, i], xin.at[n], x_s.at[n], x_r.at[n], ctx_at(0, dx))

    def z_copy(dz):
        n = ZSLOT[dz]
        return remote(zout.at[n], zin.at[n], z_s.at[n], z_r.at[n], ctx_at(dz, 0))

    arriving = {}

    def send(p):
        for i, pair in enumerate(CHUNKS[p]):
            if pair in XSLOT:
                arriving["x", pair] = x_copy(p, i)
                go(arriving["x", pair])

    def merge(pieces):
        tiles = [piece[ROWS:PIECE, :] for piece in pieces]
        peaks = [tile[0:1] for tile in tiles]
        top = functools.reduce(jnp.maximum, peaks)
        factors = [jnp.exp2(one - top) for one in peaks]
        total = functools.reduce(jnp.add, [f * tile[1:2] for f, tile in zip(factors, tiles)])
        pad = [jnp.zeros((1, HD), f32)] * (8 - len(factors))
        cols = jnp.concatenate(factors + pad, axis=0).T[0:ROWS]
        out = functools.reduce(
            jnp.add, [cols[:, i : i + 1] * piece[0:ROWS, :] for i, piece in enumerate(pieces)]
        )
        return out, jnp.concatenate([top, total, jnp.zeros((6, HD), f32)], axis=0)

    def merge_to(dst, pieces):
        out, tile = merge(pieces)
        dst[0:ROWS, :] = out
        dst[ROWS:PIECE, :] = tile

    def merge_tokens(pieces, dst):
        tiles = [piece[ROWS:PIECE, :] for piece in pieces]
        peaks = [tile[0:1] for tile in tiles]
        top = functools.reduce(jnp.maximum, peaks)
        factors = [jnp.exp2(one - top) for one in peaks]
        total = functools.reduce(jnp.add, [f * tile[1:2] for f, tile in zip(factors, tiles)])
        n = len(factors)
        pad = [jnp.zeros((1, HD), f32)] * (6 - n)
        cols = jnp.concatenate(factors + [top, total] + pad, axis=0).T[0:ROWS]
        otmp[...] = functools.reduce(
            jnp.add, [cols[:, i : i + 1] * piece[0:ROWS, :] for i, piece in enumerate(pieces)]
        )
        lane = lax.broadcasted_iota(jnp.int32, (ROWS, HD), 1)
        omax[...] = jnp.where(lane < HD // 2, cols[:, n : n + 1], cols[:, n + 1 : n + 2])
        for t in range(OWN):
            dst[t, 0:GROUP, :] = otmp[pl.ds(t, GROUP, stride=OWN), :]
            dst[t, GROUP : 2 * GROUP, :] = omax[pl.ds(t, GROUP, stride=OWN), :]

    def token_copies(n, dz):
        copies = []
        for k in range(0 if dz else 1, KVH):
            there = (g + k) % KVH
            dev = {**ctx_at(dz, 0), "kvh": there} if dz else {"kvh": there}
            copies.append(remote(osend.at[n, there], oin.at[n, g], o_s.at[n, k], o_r.at[n, k], dev))
        for copy in copies:
            copy.start()
        return copies

    where = {pair: (p, i) for p, chunk in enumerate(CHUNKS) for i, pair in enumerate(chunk)}

    def merge_x(dz):
        pieces = [part.at[where[dz, 0]]]
        for dx in (1, 2, 3):
            arriving["x", (dz, dx)].wait_recv()
            pieces.append(xin.at[XSLOT[dz, dx]])
        merge_to(zout.at[ZSLOT[dz]], pieces)

    def send_z(*dzs):
        for dz in dzs:
            arriving["z", dz] = z_copy(dz)
            go(arriving["z", dz])

    def z_wait(dz):
        arriving["z", dz].wait_recv()
        return zin.at[ZSLOT[dz]]

    def x_wait(pair):
        arriving["x", pair].wait_recv()
        return xin.at[XSLOT[pair]]

    new_copies = [
        remote(nkv.at[z], nkv.at[z], n_s.at[k - 1], n_r.at[k - 1], ctx_at(k, 0)) for k in range(1, NZ)
    ]

    for i in range(4):
        prep_part(i)
    pl.semaphore_wait(barrier, len(partners))
    own = [own_copy(dx) for dx in (1, 2, 3)]
    for copy in own:
        go(copy)
    far = {dz: far_copy(dz) for dz in (4, 3, -3)}
    for copy in far.values():
        go(copy)
    near = {(dz, dx): near_copy(dz, dx) for dz in (1, -1) for dx in range(NX)}
    go(near[1, 0])
    go(near[-1, 0])
    for dx in (1, 3, 2):
        own[dx - 1].wait_recv()
        go(near[1, dx])
        go(near[-1, dx])
    rows = {dz: row_copy(dz) for dz in (2, -2)}
    phase(0, None)
    phase(None, 0)
    passed = {(dz, dx): pass_copy(dz, dx) for dz in far for dx in (1, 2, 3)}
    for dz in far:
        far[dz].wait_recv()
        for dx in (1, 2, 3):
            go(passed[dz, dx])
    for dx in range(NX):
        near[1, dx].wait_recv()
    go(rows[2])
    phase(1, None)
    for dx in range(NX):
        near[-1, dx].wait_recv()
    go(rows[-2])
    for copy in new_copies:
        go(copy)
    phase(2, 1)
    send(1)

    def wait_passed(dz):
        for dx in (1, 2, 3):
            passed[dz, dx].wait_recv()

    wait_passed(4)
    phase(3, 2)
    send(2)
    wait_passed(3)
    phase(4, 3)
    send(3)
    for copy in new_copies:
        copy.wait_recv()
    new_keys()
    send(0)
    wait_passed(-3)
    merge_x(1)
    phase(5, 4)
    send(4)
    send_z(1)
    merge_x(-1)
    phase(None, 5)
    send(5)
    send_z(-1)
    rows[2].wait_recv()
    phase(6, None)
    merge_x(4)
    phase(None, 6)
    send(6)
    send_z(4)
    rows[-2].wait_recv()
    phase(7, None)
    merge_x(3)
    send_z(3)
    phase(None, 7)
    send(7)
    merge_x(-3)
    send_z(-3)
    pieces = [part.at[0, 0]] + [x_wait((0, dx)) for dx in (1, 2, 3)] + [z_wait(dz) for dz in (1, -1)]
    merge_to(acc1, pieces)
    def pieces_x(dz):
        return [part.at[where[dz, 0]]] + [x_wait((dz, dx)) for dx in (1, 2, 3)]

    merge_tokens(pieces_x(2), osend.at[1])
    o_copies = token_copies(1, 2)
    merge_tokens(pieces_x(-2), osend.at[2])
    o_copies += token_copies(2, -2)
    merge_tokens([acc1] + [z_wait(dz) for dz in (4, 3, -3)], osend.at[0])
    o_copies += token_copies(0, 0)
    oin[0, g] = osend[0, g]
    for copy in sent:
        copy.wait_send()
    for copy in o_copies:
        copy.wait_recv()
    outs = [oin[n, :, 0:GROUP, :].reshape(HQ, HD) for n in range(3)]
    tiles = [oin[n, :, GROUP : 2 * GROUP, :].reshape(HQ, HD) for n in range(3)]
    peaks = [tile[:, 0:1] for tile in tiles]
    top = functools.reduce(jnp.maximum, peaks)
    factors = [jnp.exp2(one - top) for one in peaks]
    total = functools.reduce(jnp.add, [f * tile[:, HD // 2 : HD // 2 + 1] for f, tile in zip(factors, tiles)])
    o_ref[...] = functools.reduce(jnp.add, [f * out for f, out in zip(factors, outs)]) / total
    for copy in o_copies:
        copy.wait_send()


def per_device(queries, cache_keys, cache_values, new_keys, new_values, block_lengths):
    vmem = pl.BlockSpec(memory_space=pltpu.VMEM)
    hbm = pl.BlockSpec(memory_space=pl.ANY)
    dma = pltpu.SemaphoreType.DMA
    out = pl.pallas_call(
        kernel,
        out_shape=jax.ShapeDtypeStruct((HQ, HD), f32),
        in_specs=[hbm, hbm, hbm, hbm, hbm, pl.BlockSpec(memory_space=pltpu.SMEM)],
        out_specs=vmem,
        scratch_shapes=[
            pltpu.VMEM((OWN, GROUP * HD), f32),
            pltpu.VMEM((BLK, HD), f32),
            pltpu.VMEM((BLK, HD), f32),
            pltpu.VMEM((BLK, 4 * HD), bf16),
            pltpu.VMEM((BLK, 2 * HD), bf16),
            pltpu.VMEM((NZ, NX, ROWS, HD), f32),
            pltpu.VMEM((NZ, 2 * OWN, HD), f32),
            pltpu.VMEM((R, BLK), f32),
            pltpu.VMEM((2, R, HD), f32),
            pltpu.VMEM((R, HD), f32),
            pltpu.VMEM((R, HD), f32),
            pltpu.VMEM((R, HD), f32),
            pltpu.VMEM((len(CHUNKS), NX, PIECE, HD), f32),
            pltpu.VMEM((len(XSLOT), PIECE, HD), f32),
            pltpu.VMEM((len(ZSLOT), PIECE, HD), f32),
            pltpu.VMEM((len(ZSLOT), PIECE, HD), f32),
            pltpu.VMEM((PIECE, HD), f32),
            pltpu.VMEM((ROWS, HD), f32),
            pltpu.VMEM((ROWS, HD), f32),
            pltpu.VMEM((3, OWN, 2 * GROUP, HD), f32),
            pltpu.VMEM((3, KVH, 2 * GROUP, HD), f32),
            dma((3,)),
            dma((4,)),
            dma((4,)),
            dma((NZ, NX)),
            dma((NZ, NX)),
            dma((NZ - 1,)),
            dma((NZ - 1,)),
            dma((len(XSLOT),)),
            dma((len(XSLOT),)),
            dma((len(ZSLOT),)),
            dma((len(ZSLOT),)),
            dma((3, KVH)),
            dma((3, KVH)),
        ],
        compiler_params=pltpu.CompilerParams(
            collective_id=0, has_side_effects=True, vmem_limit_bytes=56 * 1024 * 1024
        ),
        cost_estimate=pl.CostEstimate(
            flops=2 * 2 * 2048 * BLK * HD * 3, bytes_accessed=5 * 1024 * 1024, transcendentals=2048 * BLK
        ),
    )(queries, cache_keys, cache_values, new_keys, new_values, block_lengths)
    return out.reshape(1, HQ * HD)


def solution(mesh):
    in_specs = (P("ctx", "kvh"),) * 5 + (P("ctx"),)
    return jax.shard_map(
        per_device, mesh=mesh, in_specs=in_specs, out_specs=P(("ctx", "kvh"), None), check_vma=False
    )
```
